128 devices in a mesh: row: 32 (over z, y, core), col: 4 (over x).
Axes of the slice: x: 4, y: 4, z: 4, core: 2. Of those that a mesh axis runs over, the one named last changes fastest.
Arguments:
- panel_v: bfloat16 [2, 32, 2048, 256], P(None, 'row'), may hold values from -0.8984375 to 0.8984375
- head_v: bfloat16 [2048, 256], replicated, may hold values from -0.13183594 to 0.13183594
- head_u: bfloat16 [2048, 256], replicated, may hold values from -0.1875 to 0.1875
- diag_inverse: bfloat16 [2, 2048, 2048], P(None, 'col', 'row'), as said below
- diag_next: float32 [2048, 2048], P('row', 'col'), may hold values from -0.3 to 0.3
- ranks: int32 [2, 32], P(None, 'row'), may hold values from 64 to 256
- trail_col: int32 [32, 4, 4], P('row'), may hold values from 0 to 31
Outputs:
- panel0_factor: bfloat16 [32, 2048, 256], P('row', 'col')
- panel1_factor: bfloat16 [32, 2048, 256], P('row', 'col')
- coupling: float32 [32, 256, 256], P('row')
- head_image: bfloat16 [2048, 256], P('col')
- next_diagonal: float32 [2048, 2048], P('row', 'col')
- trail_cores: float32 [32, 4, 4, 512, 512], P('row', 'col')
The draws below stay inside these ranges and needn't reach their ends.
Inputs may be any that keep to these rules, and one draw needn't show every extreme that they name: `diag_inverse`: lower triangular, with diagonal entries between 0.5 and 2 and small entries below the diagonal.
All inputs are finite; a program needn't handle non-finite values.
Results may differ from the reference program's by a relative error of at most 0.0057.
Values may be sent and summed in bfloat16 or wider, within the bound.
No kernel may reach another device: no remote copies, remote signals or barrier semaphores. Data moves between devices by JAX's collectives and lax.ppermute only.
A program may use at most 128 MiB of HBM per device.

```python
import math
import jax
import jax.numpy as jnp
from jax import lax

NB = 2048
R = 256
TJ = 4
M = 32
N_COL = 4


def draw_diag_inverse(key, part):
    key = jax.random.fold_in(key, 7)
    first_key, second_key = jax.random.split(key)
    lower = jax.random.normal(first_key, (2, NB, NB), jnp.float32) * (0.5 / math.sqrt(NB))
    diagonal = jax.random.uniform(second_key, (2, NB), jnp.float32, 0.5, 2.0)
    places = jnp.arange(NB)
    strict = (places[:, None] > places[None, :]).astype(jnp.float32)
    unit = (places[:, None] == places[None, :]).astype(jnp.float32)
    return (lower * strict[None] + diagonal[:, :, None] * unit[None]).astype(jnp.bfloat16)


def place_ends(values, stream_key, least, top_value):
    place = [jax.random.randint(jax.random.fold_in(stream_key, axis), (), 0, length) for axis, length in enumerate(values.shape)]
    main_axis = values.shape.index(max(values.shape))
    beside = place[:main_axis] + [(place[main_axis] + 1) % values.shape[main_axis]] + place[main_axis + 1:]
    return values.at[tuple(place)].set(least).at[tuple(beside)].set(top_value)


def block_levels(key, dims, cuts, smallest, high):
    factor_of = 1.0
    for axis_at, shards_of in cuts:
        heights = jax.random.uniform(jax.random.fold_in(jax.random.fold_in(key, 6), axis_at), (shards_of,), jnp.float32, smallest / len(cuts), high / len(cuts))
        factor_of = factor_of * jnp.repeat(jnp.exp(heights), dims[axis_at] // shards_of).reshape((-1,) + (1,) * (len(dims) - 1 - axis_at))
    return factor_of


def gaussian(rng, extent, deviation, most, shards=(), held_as=jnp.bfloat16):
    values = deviation * jax.random.normal(rng, extent, jnp.float32)
    if shards:
        values = values * block_levels(rng, extent, shards, -0.22, 0.18)
    return jnp.clip(values, -most, most).astype(held_as)


def setup_inputs(seed: int = 0) -> dict:
    arg_keys = jax.random.split(jax.random.key(seed), 8)
    panel_v = gaussian(arg_keys[0], (2, M, NB, R), 0.15, 0.8984375, ((1, 32),))
    head_v = gaussian(arg_keys[1], (NB, R), (NB ** -0.5), 0.13183594)
    head_u = gaussian(arg_keys[2], (NB, R), (0.5 * R ** -0.5), 0.1875)
    diag_inverse = draw_diag_inverse(jax.random.fold_in(arg_keys[7], 71), 0)
    diag_next = gaussian(arg_keys[4], (NB, NB), 0.05, 0.3, ((0, 32), (1, 4)), jnp.float32)
    ranks = place_ends(jax.random.randint(arg_keys[5], (2, M), R // 4, R + 1), jax.random.fold_in(arg_keys[5], 1), R // 4, R).astype(jnp.int32)
    trail_col = place_ends(jax.random.randint(arg_keys[6], (M, N_COL, TJ), 0, M), jax.random.fold_in(arg_keys[6], 1), 0, M - 1).astype(jnp.int32)
    return {"panel_v": panel_v, "head_v": head_v, "head_u": head_u, "diag_inverse": diag_inverse, "diag_next": diag_next, "ranks": ranks, "trail_col": trail_col}


def apply_inverse(inverse, factors):
    count = factors.shape[0]
    flat = jnp.transpose(factors, (1, 0, 2)).reshape(NB, count * R)
    image = jnp.dot(inverse, flat, preferred_element_type=jnp.float32).astype(jnp.bfloat16)
    return jnp.transpose(image.reshape(NB, count, R), (1, 0, 2))


def reference(panel_v, head_v, head_u, diag_inverse, diag_next, ranks, trail_col):
    highest = lax.Precision.HIGHEST
    keep = (jnp.arange(R)[None, None, :] < ranks[:, :, None]).astype(jnp.bfloat16)
    masked = panel_v * keep[:, :, None, :]
    factor0 = apply_inverse(diag_inverse[0], masked[0])
    factor1 = apply_inverse(diag_inverse[1], masked[1])
    head_solved = jnp.dot(diag_inverse[0], head_v, preferred_element_type=jnp.float32).astype(jnp.bfloat16)
    head_image = jnp.dot(diag_inverse[1], head_u, preferred_element_type=jnp.float32).astype(jnp.bfloat16)
    first = factor0.astype(jnp.float32)
    second = factor1.astype(jnp.float32)
    solved32 = head_solved.astype(jnp.float32)
    image32 = head_image.astype(jnp.float32)
    coupling = jnp.einsum('mnr,ns->mrs', first, solved32, precision=highest)
    cross = jnp.einsum('mnr,ns->mrs', second, image32, precision=highest)
    gram_w = jnp.dot(head_image.T, head_image, preferred_element_type=jnp.float32)
    gram_h = jnp.dot(head_solved.T, head_solved, preferred_element_type=jnp.float32)
    upper32 = head_u.astype(jnp.float32)
    next_diagonal = diag_next - jnp.dot(jnp.dot(upper32, gram_h, precision=highest), upper32.T, precision=highest)

    def one_row(index):
        picks = trail_col[index].reshape(-1)
        pick_first = first[picks]
        pick_second = second[picks]
        pick_coupling = coupling[picks]
        own_coupling = coupling[index]
        weighted = jnp.dot(own_coupling, gram_w, precision=highest)
        block00 = jnp.einsum('nr,snq->srq', first[index], pick_first, precision=highest)
        block00 = block00 + jnp.einsum('rl,sql->srq', weighted, pick_coupling, precision=highest)
        through = jnp.einsum('nk,snq->skq', image32, pick_second, precision=highest)
        block01 = -jnp.einsum('rk,skq->srq', own_coupling, through, precision=highest)
        block10 = -jnp.einsum('rk,sqk->srq', cross[index], pick_coupling, precision=highest)
        block11 = jnp.einsum('nr,snq->srq', second[index], pick_second, precision=highest)
        top = jnp.concatenate([block00, block01], axis=2)
        bottom = jnp.concatenate([block10, block11], axis=2)
        whole = jnp.concatenate([top, bottom], axis=1)
        return whole.reshape(N_COL, TJ, 2 * R, 2 * R)

    trail_cores = lax.map(one_row, jnp.arange(M))
    return factor0, factor1, coupling, head_image, next_diagonal, trail_cores
```

```python
import jax
import jax.numpy as jnp
from jax import lax
from jax.sharding import PartitionSpec as P

BF = jnp.bfloat16
F32 = jnp.float32


def row_perm(dz, dy, dc):
    def at(z, y, c):
        return ((z % 4) * 4 + (y % 4)) * 2 + c

    return [
        (at(z, y, c), at(z + dz, y + dy, c ^ dc))
        for z in range(4)
        for y in range(4)
        for c in range(2)
    ]


def along_y(x, step):
    return lax.ppermute(x, "row", row_perm(0, step, 0))


def along_z(x, step):
    return lax.ppermute(x, "row", row_perm(step, 0, 0))


def other_core(x):
    return lax.ppermute(x, "row", row_perm(0, 0, 1))


def along_x(x, step):
    return lax.ppermute(x, "col", [(i, (i + step) % 4) for i in range(4)])


def ring(x, shift):
    before = shift(x, 1)
    after = shift(x, -1)
    half = x.shape[0] // 2
    opposite_low = shift(before[:half], 1)
    opposite_high = shift(after[half:], -1)
    return [x, before, after, opposite_low, opposite_high]


def gather_chips(x):
    first = jnp.concatenate(ring(x[0], along_y), axis=0)
    second = jnp.concatenate(ring(x[1], along_z), axis=0)
    return ring(first, along_z), ring(second, along_y)


def slot_of(distance):
    return jnp.where(distance == 0, 0, jnp.where(distance == 3, 1, jnp.where(distance == 1, 2, 3)))


def body(panel_v, head_v, head_u, diag_inverse, diag_next, ranks, trail_col):
    tile_size = panel_v.shape[2]
    rank = panel_v.shape[3]
    piece = tile_size // 4
    quarter = rank // 4
    col_id = lax.axis_index("col")
    row_id = lax.axis_index("row")
    core = row_id % 2
    my_y = (row_id // 2) % 4
    my_z = row_id // 8
    on_zero = core == 0

    def pick_core(zero, one):
        return jnp.where(on_zero, zero, one)

    keep = (jnp.arange(rank)[None, None, :] < ranks[:, :, None]).astype(BF)
    masked = (panel_v * keep[:, :, None, :])[:, 0]
    mine = pick_core(masked[0], masked[1])
    theirs = other_core(pick_core(masked[1], masked[0]))
    inv_t = jnp.transpose(diag_inverse, (0, 2, 1))
    inv_mine = pick_core(inv_t[0], inv_t[1])
    inv_theirs = other_core(pick_core(inv_t[1], inv_t[0]))
    right = jnp.concatenate(
        [pick_core(mine, theirs), pick_core(theirs, mine), pick_core(head_v, head_u)], axis=1
    )
    inv_pair = jnp.stack([pick_core(inv_mine, inv_theirs), pick_core(inv_theirs, inv_mine)])

    part0, part1 = gather_chips(inv_pair)
    blocks0 = jnp.concatenate(part0, axis=0).reshape(16, -1, piece)
    blocks1 = jnp.concatenate(part1, axis=0).reshape(16, -1, piece)
    chips = jnp.arange(16)
    slot_y = slot_of((chips % 4 - my_y) % 4)
    slot_z = slot_of((chips // 4 - my_z) % 4)
    inverse_t = jnp.concatenate(
        [blocks0[slot_z * 4 + slot_y], blocks1[slot_y * 4 + slot_z]], axis=1
    ).reshape(tile_size, piece)
    solved = lax.dot_general(
        inverse_t, right, (((0,), (0,)), ((), ())), preferred_element_type=F32
    ).astype(BF)

    passed = other_core(
        jnp.concatenate(
            [
                pick_core(solved[:, rank : 2 * rank], solved[:, :rank]),
                solved[:, 2 * rank :],
            ],
            axis=1,
        )
    )
    own = pick_core(solved[:, :rank], solved[:, rank : 2 * rank])
    factor_first = pick_core(own, passed[:, :rank])
    factor_second = pick_core(passed[:, :rank], own)
    head_image = pick_core(passed[:, rank:], solved[:, 2 * rank :])

    solved_t = jnp.transpose(solved[:, : 2 * rank]).reshape(2, rank, piece)

    def quarter_of(step):
        start = ((col_id + step) % 4) * quarter
        return lax.dynamic_slice_in_dim(solved_t, start, quarter, 1)

    thin = jnp.concatenate(
        [
            quarter_of(0),
            along_x(quarter_of(1), 1),
            along_x(quarter_of(3), -1),
            along_x(quarter_of(2), 2),
        ],
        axis=2,
    )
    gathered0, gathered1 = gather_chips(thin)

    whole = jnp.concatenate(ring(solved, along_x), axis=0)
    head = whole[:, 2 * rank :]
    small = lax.dot_general(whole, head, (((0,), (0,)), ((), ())), preferred_element_type=F32)
    small_other = other_core(small)
    small_zero = pick_core(small, small_other)
    coupling = pick_core(small_zero[:rank], small_zero[rank : 2 * rank])
    gram_h = small_zero[2 * rank :]

    def split(x):
        high = x.astype(BF)
        return high, (x - high.astype(F32)).astype(BF)

    band = tile_size // 32
    upper_band = lax.dynamic_slice_in_dim(head_u, row_id * band, band, 0)
    upper_piece = lax.dynamic_slice_in_dim(head_u, col_id * piece, piece, 0)

    def dot(a, b):
        return jnp.dot(a, b, preferred_element_type=F32)

    gram_high, gram_low = split(gram_h)
    middle_high, middle_low = split(dot(upper_band, gram_high) + dot(upper_band, gram_low))
    next_diagonal = diag_next - (
        dot(middle_high, upper_piece.T) + dot(middle_low, upper_piece.T)
    )

    pieces = gathered0 + gathered1
    products = jnp.concatenate([dot(p, whole) for p in pieces], axis=0)
    weight = []
    cross = []
    for a in range(2):
        c_mine = small[a * rank : (a + 1) * rank]
        c_other = small_other[a * rank : (a + 1) * rank]
        w = jnp.dot(
            small_other[2 * rank :], c_mine.T, precision=lax.Precision.HIGHEST
        )
        weight.append(pick_core(w, jnp.zeros_like(w)).astype(BF))
        cross.append((-c_other.T).astype(BF))
    thin_heads = products[:, 2 * rank :].astype(BF)
    direct = [products[:, a * rank : (a + 1) * rank] + dot(thin_heads, weight[a]) for a in range(2)]
    crossed = [dot(thin_heads, cross[a]) for a in range(2)]
    slabs = [
        jnp.concatenate([direct[a], crossed[a]], axis=1).astype(BF).reshape(32, quarter, 2 * rank)
        for a in range(2)
    ]
    tiles = trail_col[0]
    other_tiles = lax.ppermute(tiles.astype(F32), "row", row_perm(0, 0, 1)).astype(jnp.int32)
    picked = []
    for a in range(2):
        j = jnp.where(core == a, tiles, other_tiles)
        sy = slot_of(((j // 2) % 4 - my_y) % 4)
        sz = slot_of((j // 8 - my_z) % 4)
        place = jnp.where(j % 2 == 0, sz * 4 + sy, 16 + sy * 4 + sz)
        picked.append(slabs[a][place])
    stay = pick_core(picked[0], picked[1])
    go = pick_core(picked[1], picked[0])
    came = other_core(go)
    both = jnp.stack([pick_core(stay, came), pick_core(came, stay)], axis=1)
    landed = lax.all_to_all(both, "col", 0, 0, tiled=True)
    slots = tiles.shape[1]
    landed = landed.reshape(4, 2, slots, quarter, 2, rank)
    first = jnp.transpose(landed[:, 0], (1, 3, 4, 0, 2)).reshape(slots, 2, rank, rank)
    second = jnp.transpose(landed[:, 1], (1, 3, 4, 0, 2)).reshape(slots, 2, rank, rank)
    second = second[:, ::-1]
    cores = jnp.concatenate([first, second], axis=3).astype(F32)
    trail_cores = cores.reshape(1, 1, slots, 2 * rank, 2 * rank)
    return (
        factor_first[None],
        factor_second[None],
        coupling[None],
        head_image,
        next_diagonal,
        trail_cores,
    )


def solution(mesh):
    return jax.shard_map(
        body,
        mesh=mesh,
        in_specs=(
            P(None, "row", None, None),
            P(),
            P(),
            P(None, "col", "row"),
            P("row", "col"),
            P(None, "row"),
            P("row", None, None),
        ),
        out_specs=(
            P("row", "col", None),
            P("row", "col", None),
            P("row", None, None),
            P("col", None),
            P("row", "col"),
            P("row", "col", None, None, None),
        ),
        check_vma=False,
    )
```

```python
import jax
import jax.numpy as jnp
from jax import lax
from jax.experimental import pallas as pl
from jax.experimental.pallas import tpu as pltpu
from jax.sharding import PartitionSpec as P

BF = jnp.bfloat16
F32 = jnp.float32


def row_perm(dz, dy, dc):
    def at(z, y, c):
        return ((z % 4) * 4 + (y % 4)) * 2 + c

    return [
        (at(z, y, c), at(z + dz, y + dy, c ^ dc))
        for z in range(4)
        for y in range(4)
        for c in range(2)
    ]


def along_y(x, step):
    return lax.ppermute(x, "row", row_perm(0, step, 0))


def along_z(x, step):
    return lax.ppermute(x, "row", row_perm(step, 0, 0))


def other_core(x):
    return lax.ppermute(x, "row", row_perm(0, 0, 1))


def along_x(x, step):
    return lax.ppermute(x, "col", [(i, (i + step) % 4) for i in range(4)])


def ring(x, shift):
    before, after = lax.optimization_barrier((shift(x, 1), shift(x, -1)))
    half = x.shape[0] // 2
    opposite_low = shift(before[:half], 1)
    opposite_high = shift(after[half:], -1)
    return [x, before, after, opposite_low, opposite_high]


def gather_chips(x):
    first = jnp.concatenate(ring(x[0], along_y), axis=0)
    second = jnp.concatenate(ring(x[1], along_z), axis=0)
    return ring(first, along_z), ring(second, along_y)


def slot_of(distance):
    return jnp.where(distance == 0, 0, jnp.where(distance == 3, 1, jnp.where(distance == 1, 2, 3)))


DISTANCE = (0, 3, 1, 2)
VMEM = pl.BlockSpec(memory_space=pltpu.VMEM)
SMEM = pl.BlockSpec(memory_space=pltpu.SMEM)


def unit(size):
    rows = lax.broadcasted_iota(jnp.int32, (size, size), 0)
    cols = lax.broadcasted_iota(jnp.int32, (size, size), 1)
    return jnp.where(rows == cols, 1.0, 0.0).astype(BF)


def flip(x):
    return lax.dot_general(
        unit(x.shape[1]), x, (((1,), (1,)), ((), ())), preferred_element_type=F32
    )


def solve_kernel(where, *refs):
    pieces, (right0, right1, right2), (out, *thin), (whole, turned) = (
        refs[:10],
        refs[10:13],
        refs[13:18],
        refs[18:],
    )
    piece = out.shape[0]
    half = piece // 2
    width = whole.shape[1] // 16
    for part in range(2):
        for slow in range(4):
            for fast in range(4):
                if slow < 3:
                    ref, at = pieces[5 * part + slow], fast
                else:
                    ref, at = pieces[5 * part + 3 + fast // 2], fast % 2
                dz, dy = (slow, fast) if part == 0 else (fast, slow)
                z = lax.rem(where[0] + DISTANCE[dz], 4)
                y = lax.rem(where[1] + DISTANCE[dy], 4)
                start = pl.multiple_of((z * 4 + y) * width, width)
                whole[part * half : (part + 1) * half, pl.ds(start, width)] = ref[
                    at * half : (at + 1) * half, :
                ]
    rank = right0.shape[1]
    for n, right in enumerate((right0, right1, right2)):
        out[:, n * rank : (n + 1) * rank] = jnp.dot(
            whole[...], right[...], preferred_element_type=F32
        ).astype(BF)
    turned[...] = flip(out[:, : 2 * rank]).astype(BF)
    quarter = rank // 4
    for step in range(4):
        q = lax.rem(where[2] + step, 4)
        for a in range(2):
            start = pl.multiple_of(a * rank + q * quarter, quarter)
            thin[step][a * quarter : (a + 1) * quarter, :] = turned[pl.ds(start, quarter), :]


def solve(where, pieces, rights):
    piece = pieces[0].shape[0] // 2
    tile_size, rank = rights[0].shape
    return pl.pallas_call(
        solve_kernel,
        out_shape=[jax.ShapeDtypeStruct((piece, 3 * rank), BF)]
        + [jax.ShapeDtypeStruct((rank // 2, piece), BF)] * 4,
        in_specs=[SMEM] + [VMEM] * 13,
        out_specs=[VMEM] * 5,
        scratch_shapes=[
            pltpu.VMEM((piece, tile_size), BF),
            pltpu.VMEM((2 * rank, piece), BF),
        ],
        compiler_params=pltpu.CompilerParams(vmem_limit_bytes=40 * 2**20),
        cost_estimate=pl.CostEstimate(
            flops=2 * piece * tile_size * 3 * rank, bytes_accessed=8 * 2**20, transcendentals=0
        ),
        name="solve",
    )(where, *pieces, *rights)


def pick_kernel(places, products, mats, out, heads):
    rank = mats.shape[1]
    quarter = rank // 4
    count = places.shape[1]
    for a in range(2):
        for i in range(count):
            rows = pl.ds(pl.multiple_of(places[a, i] * quarter, quarter), quarter)
            heads[i * quarter : (i + 1) * quarter, :] = products[rows, 2 * rank :].astype(BF)
        low = jnp.dot(heads[...], mats[a], preferred_element_type=F32)
        for i in range(count):
            rows = pl.ds(pl.multiple_of(places[a, i] * quarter, quarter), quarter)
            mine = low[i * quarter : (i + 1) * quarter, :]
            out[a, i, :, :rank] = (mine[:, :rank] + products[rows, a * rank : (a + 1) * rank]).astype(BF)
            out[a, i, :, rank:] = mine[:, rank:].astype(BF)


def pick(places, products, mats):
    count = places.shape[1]
    rank = mats.shape[1]
    return pl.pallas_call(
        pick_kernel,
        out_shape=jax.ShapeDtypeStruct((2, count, rank // 4, 2 * rank), BF),
        in_specs=[SMEM, VMEM, VMEM],
        out_specs=VMEM,
        scratch_shapes=[pltpu.VMEM((count * rank // 4, rank), BF)],
        compiler_params=pltpu.CompilerParams(vmem_limit_bytes=40 * 2**20),
        cost_estimate=pl.CostEstimate(
            flops=2**29, bytes_accessed=10 * 2**20, transcendentals=0
        ),
        name="pick",
    )(places, products, mats)


def settle_kernel(landed, out):
    rank = landed.shape[4] // 2
    for p in range(2):
        x = landed[p, :, 0].reshape(rank, 2 * rank)
        direct = flip(x[:, :rank])
        crossed = flip(x[:, rank:])
        cols = slice(p * rank, (p + 1) * rank)
        out[0, :rank, cols] = direct if p == 0 else crossed
        out[0, rank:, cols] = crossed if p == 0 else direct


def settle(landed):
    _, cols, slots, quarter, width = landed.shape
    return pl.pallas_call(
        settle_kernel,
        grid=(slots,),
        out_shape=jax.ShapeDtypeStruct((slots, width, width), F32),
        in_specs=[pl.BlockSpec((2, cols, 1, quarter, width), lambda s: (0, 0, s, 0, 0))],
        out_specs=pl.BlockSpec((1, width, width), lambda s: (s, 0, 0)),
        cost_estimate=pl.CostEstimate(flops=2**30, bytes_accessed=6 * 2**20, transcendentals=0),
        name="settle",
    )(landed)


def body(panel_v, head_v, head_u, diag_inverse, diag_next, ranks, trail_col):
    tile_size = panel_v.shape[2]
    rank = panel_v.shape[3]
    piece = tile_size // 4
    quarter = rank // 4
    col_id = lax.axis_index("col")
    row_id = lax.axis_index("row")
    core = row_id % 2
    my_y = (row_id // 2) % 4
    my_z = row_id // 8
    on_zero = core == 0

    def pick_core(zero, one):
        return jnp.where(on_zero, zero, one)

    inv_mine = pick_core(diag_inverse[0], diag_inverse[1])
    inv_theirs = other_core(pick_core(diag_inverse[1], diag_inverse[0]))
    inv_pair = jnp.concatenate(
        [pick_core(inv_mine, inv_theirs), pick_core(inv_theirs, inv_mine)], axis=1
    ).reshape(2, piece // 2, -1)
    inv_pair, panel_v = lax.optimization_barrier((inv_pair, panel_v))
    part0, part1 = gather_chips(inv_pair)
    keep = (jnp.arange(rank)[None, None, :] < ranks[:, :, None]).astype(BF)
    masked = (panel_v * keep[:, :, None, :])[:, 0]
    mine = pick_core(masked[0], masked[1])
    theirs = other_core(pick_core(masked[1], masked[0]))
    rights = [pick_core(mine, theirs), pick_core(theirs, mine), pick_core(head_v, head_u)]
    where = jnp.stack([my_z, my_y, col_id]).astype(jnp.int32)
    solved, *thin_parts = solve(where, part0 + part1, rights)

    passed = other_core(
        jnp.concatenate(
            [
                pick_core(solved[:, rank : 2 * rank], solved[:, :rank]),
                solved[:, 2 * rank :],
            ],
            axis=1,
        )
    )
    own = pick_core(solved[:, :rank], solved[:, rank : 2 * rank])
    factor_first = pick_core(own, passed[:, :rank])
    factor_second = pick_core(passed[:, :rank], own)
    head_image = pick_core(passed[:, rank:], solved[:, 2 * rank :])

    thin = jnp.concatenate(
        [
            thin_parts[0],
            along_x(thin_parts[1], 1),
            along_x(thin_parts[3], -1),
            along_x(thin_parts[2], 2),
        ],
        axis=1,
    ).reshape(2, quarter, tile_size)
    gathered0, gathered1 = gather_chips(thin)

    whole = jnp.concatenate(ring(solved, along_x), axis=0)
    head = whole[:, 2 * rank :]
    small = lax.dot_general(whole, head, (((0,), (0,)), ((), ())), preferred_element_type=F32)
    small_other = other_core(small)
    small_zero = pick_core(small, small_other)
    coupling = pick_core(small_zero[:rank], small_zero[rank : 2 * rank])
    gram_h = small_zero[2 * rank :]

    def split(x):
        high = x.astype(BF)
        return high, (x - high.astype(F32)).astype(BF)

    band = tile_size // 32
    upper_band = lax.dynamic_slice_in_dim(head_u, row_id * band, band, 0)
    upper_piece = lax.dynamic_slice_in_dim(head_u, col_id * piece, piece, 0)

    def dot(a, b):
        return jnp.dot(a, b, preferred_element_type=F32)

    gram_high, gram_low = split(gram_h)
    middle_high, middle_low = split(dot(upper_band, gram_high) + dot(upper_band, gram_low))
    next_diagonal = diag_next - (
        dot(middle_high, upper_piece.T) + dot(middle_low, upper_piece.T)
    )

    pieces = gathered0 + gathered1
    products = jnp.concatenate([dot(p, whole) for p in pieces], axis=0)
    mats = []
    for a in range(2):
        c_mine = small[a * rank : (a + 1) * rank]
        c_other = small_other[a * rank : (a + 1) * rank]
        w = jnp.dot(small_other[2 * rank :], c_mine.T, precision=lax.Precision.HIGHEST)
        mats.append(
            jnp.concatenate([pick_core(w, jnp.zeros_like(w)), -c_other.T], axis=1).astype(BF)
        )
    tiles = trail_col[0]
    slots = tiles.shape[1]
    other_tiles = other_core(tiles.astype(F32)).astype(jnp.int32)
    j = jnp.stack([pick_core(tiles, other_tiles), pick_core(other_tiles, tiles)]).reshape(2, -1)
    sy = slot_of(((j // 2) % 4 - my_y) % 4)
    sz = slot_of((j // 8 - my_z) % 4)
    places = jnp.where(j % 2 == 0, sz * 4 + sy, 16 + sy * 4 + sz)
    picked = pick(places, products, jnp.stack(mats))
    chip_groups = [[(2 * chip + m) * 4 + c for m in range(2) for c in range(4)] for chip in range(16)]
    landed = lax.all_to_all(
        picked.reshape(8, slots, quarter, 2 * rank),
        ("row", "col"),
        0,
        0,
        axis_index_groups=chip_groups,
        tiled=True,
    )
    cores = settle(landed.reshape(2, 4, slots, quarter, 2 * rank))
    trail_cores = cores.reshape(1, 1, slots, 2 * rank, 2 * rank)
    return (
        factor_first[None],
        factor_second[None],
        coupling[None],
        head_image,
        next_diagonal,
        trail_cores,
    )


def solution(mesh):
    return jax.shard_map(
        body,
        mesh=mesh,
        in_specs=(
            P(None, "row", None, None),
            P(),
            P(),
            P(None, "col", "row"),
            P("row", "col"),
            P(None, "row"),
            P("row", None, None),
        ),
        out_specs=(
            P("row", "col", None),
            P("row", "col", None),
            P("row", None, None),
            P("col", None),
            P("row", "col"),
            P("row", "col", None, None, None),
        ),
        check_vma=False,
    )
```

```python
import jax
import jax.numpy as jnp
from jax import lax
from jax.experimental import pallas as pl
from jax.experimental.pallas import tpu as pltpu
from jax.sharding import PartitionSpec as P

BF = jnp.bfloat16
F32 = jnp.float32


def row_at(z, y, core):
    return ((z % 4) * 4 + (y % 4)) * 2 + core


def other_core(x):
    pairs = [(row_at(z, y, k), row_at(z, y, 1 - k)) for z in range(4) for y in range(4) for k in range(2)]
    return lax.ppermute(x, "row", pairs)


def along_x(x, step):
    pairs = []
    for row in range(32):
        for c in range(4):
            d = step if row % 2 == 0 else -step
            pairs.append((row * 4 + c, row * 4 + (c + d) % 4))
    return lax.ppermute(x, ("row", "col"), pairs)


def hop(x, level, step):
    pairs = []
    for z in range(4):
        for y in range(4):
            for k in range(2):
                dz = step if k != level else 0
                dy = step if k == level else 0
                pairs.append((row_at(z, y, k), row_at(z + dz, y + dy, k)))
    return lax.ppermute(x, "row", pairs)


def slot_of(distance):
    return jnp.where(distance % 2 == 0, distance // 2 * 3, jnp.where(distance == 3, 1, 2))


DISTANCE = (0, 3, 1, 2)
VMEM = pl.BlockSpec(memory_space=pltpu.VMEM)
SMEM = pl.BlockSpec(memory_space=pltpu.SMEM)
ANY = pl.BlockSpec(memory_space=pl.ANY)
HBM = pl.BlockSpec(memory_space=pltpu.HBM)


def unit(size):
    rows = lax.broadcasted_iota(jnp.int32, (size, size), 0)
    cols = lax.broadcasted_iota(jnp.int32, (size, size), 1)
    return jnp.where(rows == cols, 1.0, 0.0).astype(BF)


def flip(x):
    return lax.dot_general(
        unit(x.shape[1]), x, (((1,), (1,)), ((), ())), preferred_element_type=F32
    )


def copy_all(pairs, sems, base=0):
    copies = [pltpu.make_async_copy(src, dst, sems.at[base + i]) for i, (src, dst) in enumerate(pairs)]
    for copy in copies:
        copy.start()
    return copies


def solve_kernel(where, *refs):
    pieces, (right0, right1, right2), (out, *thin), (whole, turned) = (
        refs[:4],
        refs[4:7],
        refs[7:12],
        refs[12:],
    )
    piece = out.shape[0]
    width = whole.shape[1] // 16
    on_zero = where[3] == 0
    for slow in range(4):
        for fast in range(4):
            dz = jnp.where(on_zero, DISTANCE[slow], DISTANCE[fast])
            dy = jnp.where(on_zero, DISTANCE[fast], DISTANCE[slow])
            chip = lax.rem(where[0] + dz, 4) * 4 + lax.rem(where[1] + dy, 4)
            start = pl.multiple_of(chip * width, width)
            whole[:, pl.ds(start, width)] = pieces[slow][fast * piece : (fast + 1) * piece, :]
    rank = right0.shape[1]
    for n, right in enumerate((right0, right1, right2)):
        out[:, n * rank : (n + 1) * rank] = jnp.dot(
            whole[...], right[...], preferred_element_type=F32
        ).astype(BF)
    turned[...] = flip(out[:, : 2 * rank]).astype(BF)
    quarter = rank // 4
    half = quarter // 2
    for step in range(4):
        q = lax.rem(where[2] + jnp.where(on_zero, step, 4 - step), 4)
        for h in range(2):
            for a in range(2):
                start = pl.multiple_of(a * rank + q * quarter + h * half, half)
                at = (2 * h + a) * half
                thin[step][at : at + half, :] = turned[pl.ds(start, half), :]


def solve(where, pieces, rights):
    piece = pieces[0].shape[0] // 4
    tile_size, rank = rights[0].shape
    return pl.pallas_call(
        solve_kernel,
        out_shape=[jax.ShapeDtypeStruct((piece, 3 * rank), BF)]
        + [jax.ShapeDtypeStruct((rank // 2, piece), BF)] * 4,
        in_specs=[SMEM] + [VMEM] * 7,
        out_specs=[VMEM] * 5,
        scratch_shapes=[
            pltpu.VMEM((piece, tile_size), BF),
            pltpu.VMEM((2 * rank, piece), BF),
        ],
        compiler_params=pltpu.CompilerParams(vmem_limit_bytes=16 * 2**20),
        cost_estimate=pl.CostEstimate(
            flops=2 * piece * tile_size * 3 * rank, bytes_accessed=0, transcendentals=0
        ),
        name="solve",
    )(where, *pieces, *rights)


def multiply_kernel(*refs):
    count = len(refs) - 4
    whole, pieces, (out, held, sems) = refs[0], refs[1 : 1 + count], refs[1 + count :]
    rows = pieces[0].shape[0]
    copies = copy_all(
        [(p, held.at[pl.ds(i * rows, rows)]) for i, p in enumerate(pieces)], sems
    )
    for copy in copies:
        copy.wait()
    out[...] = jnp.dot(held[...], whole[...], preferred_element_type=F32)


def multiply(whole, pieces):
    depth, width = whole.shape
    rows = pieces[0].shape[0]
    count = len(pieces)
    return pl.pallas_call(
        multiply_kernel,
        out_shape=jax.ShapeDtypeStruct((count * rows, width), F32),
        in_specs=[VMEM] + [ANY] * count,
        out_specs=VMEM,
        scratch_shapes=[
            pltpu.VMEM((count * rows, depth), BF),
            pltpu.SemaphoreType.DMA((count,)),
        ],
        compiler_params=pltpu.CompilerParams(vmem_limit_bytes=16 * 2**20),
        cost_estimate=pl.CostEstimate(
            flops=2 * count * rows * depth * width, bytes_accessed=0, transcendentals=0
        ),
        name="multiply",
    )(whole, *pieces)


def pick_kernel(
    places, mats, whole, piece0, piece1, early0, early1, out, late0, late1, heads, staged, sems
):
    done = early0.shape[0]
    copies = copy_all(
        [(early0, late0.at[pl.ds(0, done)]), (early1, late1.at[pl.ds(0, done)])], sems, 2
    )
    late0[done:, :] = jnp.dot(piece0[...], whole[...], preferred_element_type=F32)
    late1[done:, :] = jnp.dot(piece1[...], whole[...], preferred_element_type=F32)
    for copy in copies:
        copy.wait()
    products = (late0, late1)
    rank = mats.shape[1]
    half = rank // 8
    count = places.shape[1]
    leaving = []
    for a in range(2):
        at = [pl.ds(pl.multiple_of(places[a, i] * half, half), half) for i in range(count)]
        for i in range(count):
            for h in range(2):
                rows = slice((2 * i + h) * half, (2 * i + h + 1) * half)
                heads[rows, :] = products[h][at[i], 2 * rank :].astype(BF)
        low = jnp.dot(heads[...], mats[a], preferred_element_type=F32)
        for i in range(count):
            for h in range(2):
                mine = low[(2 * i + h) * half : (2 * i + h + 1) * half, :]
                direct = products[h][at[i], a * rank : (a + 1) * rank]
                rows = slice(h * half, (h + 1) * half)
                staged[a, i, rows, :rank] = (mine[:, :rank] + direct).astype(BF)
                staged[a, i, rows, rank:] = mine[:, rank:].astype(BF)
        leaving += copy_all([(staged.at[a], out.at[a])], sems, a)
    for copy in leaving:
        copy.wait()


def pick(places, mats, whole, piece0, piece1, early0, early1):
    count = places.shape[1]
    rank = mats.shape[1]
    shape = (2, count, rank // 4, 2 * rank)
    full = (early0.shape[0] + piece0.shape[0], early0.shape[1])
    return pl.pallas_call(
        pick_kernel,
        out_shape=jax.ShapeDtypeStruct(shape, BF),
        in_specs=[SMEM] + [VMEM] * 6,
        out_specs=HBM,
        scratch_shapes=[
            pltpu.VMEM(full, F32),
            pltpu.VMEM(full, F32),
            pltpu.VMEM((count * rank // 4, rank), BF),
            pltpu.VMEM(shape, BF),
            pltpu.SemaphoreType.DMA((4,)),
        ],
        compiler_params=pltpu.CompilerParams(vmem_limit_bytes=28 * 2**20),
        cost_estimate=pl.CostEstimate(
            flops=2**30, bytes_accessed=0, transcendentals=0
        ),
        name="pick",
    )(places, mats, whole, piece0, piece1, early0, early1)


def couple_kernel(*refs):
    parts, whole, out = refs[:4], refs[4], refs[5]
    rank = out.shape[1]
    size = parts[0].shape[0]
    for i, part in enumerate(parts):
        whole[i * size : (i + 1) * size, :] = part[...]
        term = lax.dot_general(
            part[...], part[:, 2 * rank :], (((0,), (0,)), ((), ())), preferred_element_type=F32
        )
        out[...] = term if i == 0 else out[...] + term


def couple(parts):
    size, width = parts[0].shape
    return pl.pallas_call(
        couple_kernel,
        out_shape=[
            jax.ShapeDtypeStruct((4 * size, width), BF),
            jax.ShapeDtypeStruct((width, width // 3), F32),
        ],
        in_specs=[VMEM] * 4,
        out_specs=[VMEM] * 2,
        compiler_params=pltpu.CompilerParams(vmem_limit_bytes=16 * 2**20),
        cost_estimate=pl.CostEstimate(
            flops=2 * 4 * size * width * width // 3, bytes_accessed=0, transcendentals=0
        ),
        name="couple",
    )(*parts)


def split(x):
    high = x.astype(BF)
    return high, (x - high.astype(F32)).astype(BF)


def by_rows(a, b):
    return lax.dot_general(a, b, (((1,), (1,)), ((), ())), preferred_element_type=F32)


def finish_kernel(core, small, other, mats, coupling, gram):
    rank = small.shape[1]
    last = slice(2 * rank, 3 * rank)
    on_zero = core[0] == 0
    for a in range(2):
        rows = slice(a * rank, (a + 1) * rank)
        high, low = split(small[rows, :])
        gram_high, gram_low = split(other[last, :])
        weight = by_rows(gram_high, high) + by_rows(gram_high, low) + by_rows(gram_low, high)
        mats[a, :, :rank] = jnp.where(on_zero, weight, 0.0).astype(BF)
        mats[a, :, rank:] = (-flip(other[rows, :].astype(BF))).astype(BF)
    coupling[...] = jnp.where(on_zero, small[:rank, :], other[rank : 2 * rank, :])
    gram[...] = jnp.where(on_zero, small[last, :], other[last, :])


def finish(core, small, other):
    rank = small.shape[1]
    return pl.pallas_call(
        finish_kernel,
        out_shape=[
            jax.ShapeDtypeStruct((2, rank, 2 * rank), BF),
            jax.ShapeDtypeStruct((rank, rank), F32),
            jax.ShapeDtypeStruct((rank, rank), F32),
        ],
        in_specs=[SMEM] + [VMEM] * 2,
        out_specs=[VMEM] * 3,
        compiler_params=pltpu.CompilerParams(vmem_limit_bytes=8 * 2**20),
        cost_estimate=pl.CostEstimate(flops=2**28, bytes_accessed=0, transcendentals=0),
        name="finish",
    )(core, small, other)


def update_kernel(gram, band, piece, before, after):
    gram_high, gram_low = split(gram[...])
    middle = jnp.dot(band[...], gram_high, preferred_element_type=F32) + jnp.dot(
        band[...], gram_low, preferred_element_type=F32
    )
    high, low = split(middle)
    after[...] = before[...] - (by_rows(high, piece[...]) + by_rows(low, piece[...]))


def update(gram, band, piece, before):
    return pl.pallas_call(
        update_kernel,
        out_shape=jax.ShapeDtypeStruct(before.shape, F32),
        in_specs=[VMEM] * 4,
        out_specs=VMEM,
        compiler_params=pltpu.CompilerParams(vmem_limit_bytes=8 * 2**20),
        cost_estimate=pl.CostEstimate(flops=2**26, bytes_accessed=0, transcendentals=0),
        name="update",
    )(gram, band, piece, before)


def settle_kernel(landed, out):
    rank = landed.shape[4] // 2
    for p in range(2):
        x = landed[p, :, pl.program_id(0)].reshape(rank, 2 * rank)
        direct = flip(x[:, :rank])
        crossed = flip(x[:, rank:])
        cols = slice(p * rank, (p + 1) * rank)
        out[0, :rank, cols] = direct if p == 0 else crossed
        out[0, rank:, cols] = crossed if p == 0 else direct


def settle(landed):
    slots, width = landed.shape[2], landed.shape[4]
    return pl.pallas_call(
        settle_kernel,
        grid=(slots,),
        out_shape=jax.ShapeDtypeStruct((slots, width, width), F32),
        in_specs=[VMEM],
        out_specs=pl.BlockSpec((1, width, width), lambda s: (s, 0, 0)),
        compiler_params=pltpu.CompilerParams(vmem_limit_bytes=16 * 2**20),
        cost_estimate=pl.CostEstimate(flops=2**30, bytes_accessed=0, transcendentals=0),
        name="settle",
    )(landed)


def join_kernel(*refs):
    pieces, outs = refs[:4], refs[4:]
    rows = pieces[0].shape[0] // len(outs)
    for n, out in enumerate(outs):
        for i in range(4):
            out[i * rows : (i + 1) * rows, :] = pieces[i][n * rows : (n + 1) * rows, :]


def join(pieces, count):
    rows, cols = pieces[0].shape
    return pl.pallas_call(
        join_kernel,
        out_shape=[jax.ShapeDtypeStruct((4 * rows // count, cols), BF)] * count,
        in_specs=[VMEM] * 4,
        out_specs=[VMEM] * count,
        compiler_params=pltpu.CompilerParams(vmem_limit_bytes=8 * 2**20),
        cost_estimate=pl.CostEstimate(
            flops=0, bytes_accessed=0, transcendentals=0
        ),
        name="join",
    )(*pieces)


def direct(x, level):
    return [x, hop(x, level, 1), hop(x, level, -1), hop(x, level, 2)]


def sides(x, level):
    return hop(x, level, 1), hop(x, level, -1)


def body(panel_v, head_v, head_u, diag_inverse, diag_next, ranks, trail_col):
    tile_size = panel_v.shape[2]
    rank = panel_v.shape[3]
    piece = tile_size // 4
    quarter = rank // 4
    col_id = lax.axis_index("col")
    row_id = lax.axis_index("row")
    core = row_id % 2
    my_y = (row_id // 2) % 4
    my_z = row_id // 8
    on_zero = core == 0

    def pick_core(zero, one):
        return jnp.where(on_zero, zero, one)

    inv_mine = pick_core(diag_inverse[0], diag_inverse[1])
    inv_theirs = other_core(pick_core(diag_inverse[1], diag_inverse[0]))
    inv_pair = jnp.concatenate(
        [pick_core(inv_mine, inv_theirs), pick_core(inv_theirs, inv_mine)], axis=1
    )
    column = join(direct(inv_pair, 0), 1)[0]
    panel_other = other_core(panel_v)
    column, panel_late, ranks, trail_col = lax.optimization_barrier((column, panel_v, ranks, trail_col))
    inverse = direct(column, 1)
    own_core = core.astype(jnp.int32)[None]
    cols = jnp.arange(rank)[None, :]
    tiles = trail_col[0]
    slots = tiles.shape[1]
    numbers = jnp.concatenate([ranks[:, 0], tiles.reshape(-1)])
    numbers_other = other_core(numbers.astype(F32)[None])[0].astype(jnp.int32)

    def masked(panels, limits):
        kept = [jnp.where(cols < limits[p], panels[p, 0], jnp.zeros((), BF)) for p in range(2)]
        return pick_core(*kept)

    mine = masked(panel_late, numbers)
    theirs = masked(panel_other, numbers_other)
    rights = [pick_core(mine, theirs), pick_core(theirs, mine), pick_core(head_v, head_u)]
    where = jnp.stack([my_z, my_y, col_id, core]).astype(jnp.int32)
    solved, *thin_parts = solve(where, inverse, rights)

    thin_before = along_x(thin_parts[1], 1)
    thin_after = along_x(thin_parts[3], -1)
    thin_opposite = along_x(thin_parts[2], 2)
    thin_before, thin_after, sent = lax.optimization_barrier((thin_before, thin_after, solved))
    thin = jnp.concatenate([thin_parts[0], thin_before, thin_after, thin_opposite], axis=1)
    quarters = thin.reshape(2, quarter, tile_size)
    line0, line1 = (join(direct(quarters[h], 0), 1)[0] for h in range(2))
    x_before, x_after, x_opposite = along_x(sent, 1), along_x(sent, -1), along_x(sent, 2)
    line1, x_before, x_after, x_opposite = lax.optimization_barrier(
        (line1, x_before, x_after, x_opposite)
    )
    before0, after0 = lax.optimization_barrier(sides(line0, 1))
    before1, after1 = lax.optimization_barrier(sides(line1, 1))
    gathered0 = [line0, before0, after0, hop(before0, 1, 1)]
    whole, small = couple([solved, x_before, x_after, x_opposite])
    early0 = multiply(whole, gathered0[:3])
    after1, small, early0 = lax.optimization_barrier((after1, small, early0))
    gathered1 = [line1, before1, after1, hop(after1, 1, -1)]
    small_other = other_core(small)
    mats, coupling, gram_h = finish(own_core, small, small_other)

    late, _ = lax.optimization_barrier((solved, gathered0[1]))
    passed = other_core(
        jnp.concatenate(
            [
                pick_core(late[:, rank : 2 * rank], late[:, :rank]),
                late[:, 2 * rank :],
            ],
            axis=1,
        )
    )
    own = pick_core(late[:, :rank], late[:, rank : 2 * rank])
    factor_first = pick_core(own, passed[:, :rank])
    factor_second = pick_core(passed[:, :rank], own)
    head_image = pick_core(passed[:, rank:], late[:, 2 * rank :])

    other_tiles = numbers_other[2:].reshape(tiles.shape)
    j = jnp.stack([pick_core(tiles, other_tiles), pick_core(other_tiles, tiles)]).reshape(2, -1)
    sy = slot_of(((j // 2) % 4 - my_y) % 4)
    sz = slot_of((j // 8 - my_z) % 4)
    places = (pick_core(sz, sy) * 4 + pick_core(sy, sz)) * 2 + j % 2
    early1 = multiply(whole, gathered1[:3])
    picked = pick(places, mats, whole, gathered0[3], gathered1[3], early0, early1)
    upper, _ = lax.optimization_barrier((head_u, picked))
    band = tile_size // 32
    upper_band = lax.dynamic_slice_in_dim(upper, row_id * band, band, 0)
    upper_piece = lax.dynamic_slice_in_dim(upper, col_id * piece, piece, 0)
    next_diagonal = update(gram_h, upper_band, upper_piece, diag_next)
    chip_groups = [[(2 * chip + m) * 4 + c for m in range(2) for c in range(4)] for chip in range(16)]
    landed = lax.all_to_all(
        picked.reshape(8, slots, quarter, 2 * rank),
        ("row", "col"),
        0,
        0,
        axis_index_groups=chip_groups,
        tiled=True,
    )
    cores = settle(landed.reshape(2, 4, slots, quarter, 2 * rank))
    trail_cores = cores.reshape(1, 1, slots, 2 * rank, 2 * rank)
    return (
        factor_first[None],
        factor_second[None],
        coupling[None],
        head_image,
        next_diagonal,
        trail_cores,
    )


def solution(mesh):
    return jax.shard_map(
        body,
        mesh=mesh,
        in_specs=(
            P(None, "row", None, None),
            P(),
            P(),
            P(None, "col", "row"),
            P("row", "col"),
            P(None, "row"),
            P("row", None, None),
        ),
        out_specs=(
            P("row", "col", None),
            P("row", "col", None),
            P("row", None, None),
            P("col", None),
            P("row", "col"),
            P("row", "col", None, None, None),
        ),
        check_vma=False,
    )
```

```python
import jax
import jax.numpy as jnp
from jax import lax
from jax.experimental import pallas as pl
from jax.experimental.pallas import tpu as pltpu
from jax.sharding import PartitionSpec as P

BF = jnp.bfloat16
F32 = jnp.float32


def row_at(z, y, core):
    return ((z % 4) * 4 + (y % 4)) * 2 + core


def other_core(x):
    pairs = [(row_at(z, y, k), row_at(z, y, 1 - k)) for z in range(4) for y in range(4) for k in range(2)]
    return lax.ppermute(x, "row", pairs)


def along_x(x, step):
    pairs = []
    for row in range(32):
        for c in range(4):
            d = step if row % 2 == 0 else -step
            pairs.append((row * 4 + c, row * 4 + (c + d) % 4))
    return lax.ppermute(x, ("row", "col"), pairs)


def hop(x, level, step):
    pairs = []
    for z in range(4):
        for y in range(4):
            for k in range(2):
                dz = step if k != level else 0
                dy = step if k == level else 0
                pairs.append((row_at(z, y, k), row_at(z + dz, y + dy, k)))
    return lax.ppermute(x, "row", pairs)


def slot_of(distance):
    return jnp.where(distance % 2 == 0, distance // 2 * 3, jnp.where(distance == 3, 1, 2))


DISTANCE = (0, 3, 1, 2)
VMEM = pl.BlockSpec(memory_space=pltpu.VMEM)
SMEM = pl.BlockSpec(memory_space=pltpu.SMEM)
ANY = pl.BlockSpec(memory_space=pl.ANY)
HBM = pl.BlockSpec(memory_space=pltpu.HBM)


def unit(size):
    rows = lax.broadcasted_iota(jnp.int32, (size, size), 0)
    cols = lax.broadcasted_iota(jnp.int32, (size, size), 1)
    return jnp.where(rows == cols, 1.0, 0.0).astype(BF)


def flip(x):
    return lax.dot_general(
        unit(x.shape[1]), x, (((1,), (1,)), ((), ())), preferred_element_type=F32
    )


def copy_all(pairs, sems, base=0):
    copies = [pltpu.make_async_copy(src, dst, sems.at[base + i]) for i, (src, dst) in enumerate(pairs)]
    for copy in copies:
        copy.start()
    return copies


def solve_kernel(where, *refs):
    pieces, (right0, right1, right2), (out, *thin), (whole, turned) = (
        refs[:4],
        refs[4:7],
        refs[7:12],
        refs[12:],
    )
    piece = out.shape[0]
    width = whole.shape[1] // 16
    on_zero = where[3] == 0
    for slow in range(4):
        for fast in range(4):
            dz = jnp.where(on_zero, DISTANCE[slow], DISTANCE[fast])
            dy = jnp.where(on_zero, DISTANCE[fast], DISTANCE[slow])
            chip = lax.rem(where[0] + dz, 4) * 4 + lax.rem(where[1] + dy, 4)
            start = pl.multiple_of(chip * width, width)
            whole[:, pl.ds(start, width)] = pieces[slow][fast * piece : (fast + 1) * piece, :]
    rank = right0.shape[1]
    for n, right in enumerate((right0, right1, right2)):
        out[:, n * rank : (n + 1) * rank] = jnp.dot(
            whole[...], right[...], preferred_element_type=F32
        ).astype(BF)
    turned[...] = flip(out[:, : 2 * rank]).astype(BF)
    quarter = rank // 4
    half = quarter // 2
    for step in range(4):
        q = lax.rem(where[2] + jnp.where(on_zero, step, 4 - step), 4)
        for h in range(2):
            for a in range(2):
                start = pl.multiple_of(a * rank + q * quarter + h * half, half)
                at = (2 * h + a) * half
                thin[step][at : at + half, :] = turned[pl.ds(start, half), :]


def solve(where, pieces, rights):
    piece = pieces[0].shape[0] // 4
    tile_size, rank = rights[0].shape
    return pl.pallas_call(
        solve_kernel,
        out_shape=[jax.ShapeDtypeStruct((piece, 3 * rank), BF)]
        + [jax.ShapeDtypeStruct((rank // 2, piece), BF)] * 4,
        in_specs=[SMEM] + [VMEM] * 7,
        out_specs=[VMEM] * 5,
        scratch_shapes=[
            pltpu.VMEM((piece, tile_size), BF),
            pltpu.VMEM((2 * rank, piece), BF),
        ],
        compiler_params=pltpu.CompilerParams(vmem_limit_bytes=16 * 2**20),
        cost_estimate=pl.CostEstimate(
            flops=2 * piece * tile_size * 3 * rank, bytes_accessed=0, transcendentals=0
        ),
        name="solve",
    )(where, *pieces, *rights)


def multiply_kernel(*refs):
    count = len(refs) - 4
    whole, pieces, (out, held, sems) = refs[0], refs[1 : 1 + count], refs[1 + count :]
    rows = pieces[0].shape[0]
    copies = copy_all(
        [(p, held.at[pl.ds(i * rows, rows)]) for i, p in enumerate(pieces)], sems
    )
    for copy in copies:
        copy.wait()
    out[...] = jnp.dot(held[...], whole[...], preferred_element_type=F32)


def multiply(whole, pieces):
    depth, width = whole.shape
    rows = pieces[0].shape[0]
    count = len(pieces)
    return pl.pallas_call(
        multiply_kernel,
        out_shape=jax.ShapeDtypeStruct((count * rows, width), F32),
        in_specs=[VMEM] + [ANY] * count,
        out_specs=VMEM,
        scratch_shapes=[
            pltpu.VMEM((count * rows, depth), BF),
            pltpu.SemaphoreType.DMA((count,)),
        ],
        compiler_params=pltpu.CompilerParams(vmem_limit_bytes=16 * 2**20),
        cost_estimate=pl.CostEstimate(
            flops=2 * count * rows * depth * width, bytes_accessed=0, transcendentals=0
        ),
        name="multiply",
    )(whole, *pieces)


def pick_kernel(
    places, mats, whole, piece0, piece1, early0, early1, out, late0, late1, heads, staged, sems
):
    done = early0.shape[0]
    copies = copy_all(
        [(early0, late0.at[pl.ds(0, done)]), (early1, late1.at[pl.ds(0, done)])], sems, 2
    )
    late0[done:, :] = jnp.dot(piece0[...], whole[...], preferred_element_type=F32)
    late1[done:, :] = jnp.dot(piece1[...], whole[...], preferred_element_type=F32)
    for copy in copies:
        copy.wait()
    products = (late0, late1)
    rank = mats.shape[1]
    half = rank // 8
    count = places.shape[1]
    leaving = []
    for a in range(2):
        at = [pl.ds(pl.multiple_of(places[a, i] * half, half), half) for i in range(count)]
        for i in range(count):
            for h in range(2):
                rows = slice((2 * i + h) * half, (2 * i + h + 1) * half)
                heads[rows, :] = products[h][at[i], 2 * rank :].astype(BF)
        low = jnp.dot(heads[...], mats[a], preferred_element_type=F32)
        for i in range(count):
            for h in range(2):
                mine = low[(2 * i + h) * half : (2 * i + h + 1) * half, :]
                direct = products[h][at[i], a * rank : (a + 1) * rank]
                rows = slice(h * half, (h + 1) * half)
                staged[a, i, rows, :rank] = (mine[:, :rank] + direct).astype(BF)
                staged[a, i, rows, rank:] = mine[:, rank:].astype(BF)
        leaving += copy_all([(staged.at[a], out.at[a])], sems, a)
    for copy in leaving:
        copy.wait()


def pick(places, mats, whole, piece0, piece1, early0, early1):
    count = places.shape[1]
    rank = mats.shape[1]
    shape = (2, count, rank // 4, 2 * rank)
    full = (early0.shape[0] + piece0.shape[0], early0.shape[1])
    return pl.pallas_call(
        pick_kernel,
        out_shape=jax.ShapeDtypeStruct(shape, BF),
        in_specs=[SMEM] + [VMEM] * 6,
        out_specs=HBM,
        scratch_shapes=[
            pltpu.VMEM(full, F32),
            pltpu.VMEM(full, F32),
            pltpu.VMEM((count * rank // 4, rank), BF),
            pltpu.VMEM(shape, BF),
            pltpu.SemaphoreType.DMA((4,)),
        ],
        compiler_params=pltpu.CompilerParams(vmem_limit_bytes=28 * 2**20),
        cost_estimate=pl.CostEstimate(
            flops=2**30, bytes_accessed=0, transcendentals=0
        ),
        name="pick",
    )(places, mats, whole, piece0, piece1, early0, early1)


def couple_kernel(*refs):
    parts, whole, out = refs[:4], refs[4], refs[5]
    rank = out.shape[1]
    size = parts[0].shape[0]
    for i, part in enumerate(parts):
        whole[i * size : (i + 1) * size, :] = part[...]
        term = lax.dot_general(
            part[...], part[:, 2 * rank :], (((0,), (0,)), ((), ())), preferred_element_type=F32
        )
        out[...] = term if i == 0 else out[...] + term


def couple(parts):
    size, width = parts[0].shape
    return pl.pallas_call(
        couple_kernel,
        out_shape=[
            jax.ShapeDtypeStruct((4 * size, width), BF),
            jax.ShapeDtypeStruct((width, width // 3), F32),
        ],
        in_specs=[VMEM] * 4,
        out_specs=[VMEM] * 2,
        compiler_params=pltpu.CompilerParams(vmem_limit_bytes=16 * 2**20),
        cost_estimate=pl.CostEstimate(
            flops=2 * 4 * size * width * width // 3, bytes_accessed=0, transcendentals=0
        ),
        name="couple",
    )(*parts)


def split(x):
    high = x.astype(BF)
    return high, (x - high.astype(F32)).astype(BF)


def by_rows(a, b):
    return lax.dot_general(a, b, (((1,), (1,)), ((), ())), preferred_element_type=F32)


def finish_kernel(core, small, other, mats, coupling, gram):
    rank = small.shape[1]
    last = slice(2 * rank, 3 * rank)
    on_zero = core[0] == 0
    for a in range(2):
        rows = slice(a * rank, (a + 1) * rank)
        high, low = split(small[rows, :])
        gram_high, gram_low = split(other[last, :])
        weight = by_rows(gram_high, high) + by_rows(gram_high, low) + by_rows(gram_low, high)
        mats[a, :, :rank] = jnp.where(on_zero, weight, 0.0).astype(BF)
        mats[a, :, rank:] = (-flip(other[rows, :].astype(BF))).astype(BF)
    coupling[...] = jnp.where(on_zero, small[:rank, :], other[rank : 2 * rank, :])
    gram[...] = jnp.where(on_zero, small[last, :], other[last, :])


def finish(core, small, other):
    rank = small.shape[1]
    return pl.pallas_call(
        finish_kernel,
        out_shape=[
            jax.ShapeDtypeStruct((2, rank, 2 * rank), BF),
            jax.ShapeDtypeStruct((rank, rank), F32),
            jax.ShapeDtypeStruct((rank, rank), F32),
        ],
        in_specs=[SMEM] + [VMEM] * 2,
        out_specs=[VMEM] * 3,
        compiler_params=pltpu.CompilerParams(vmem_limit_bytes=8 * 2**20),
        cost_estimate=pl.CostEstimate(flops=2**28, bytes_accessed=0, transcendentals=0),
        name="finish",
    )(core, small, other)


def update_kernel(gram, band, piece, before, after):
    gram_high, gram_low = split(gram[...])
    middle = jnp.dot(band[...], gram_high, preferred_element_type=F32) + jnp.dot(
        band[...], gram_low, preferred_element_type=F32
    )
    high, low = split(middle)
    after[...] = before[...] - (by_rows(high, piece[...]) + by_rows(low, piece[...]))


def update(gram, band, piece, before):
    return pl.pallas_call(
        update_kernel,
        out_shape=jax.ShapeDtypeStruct(before.shape, F32),
        in_specs=[VMEM] * 4,
        out_specs=VMEM,
        compiler_params=pltpu.CompilerParams(vmem_limit_bytes=8 * 2**20),
        cost_estimate=pl.CostEstimate(flops=2**26, bytes_accessed=0, transcendentals=0),
        name="update",
    )(gram, band, piece, before)


def settle_kernel(landed, out):
    rank = landed.shape[4] // 2
    for p in range(2):
        x = landed[p, :, pl.program_id(0)].reshape(rank, 2 * rank)
        direct = flip(x[:, :rank])
        crossed = flip(x[:, rank:])
        cols = slice(p * rank, (p + 1) * rank)
        out[0, :rank, cols] = direct if p == 0 else crossed
        out[0, rank:, cols] = crossed if p == 0 else direct


def settle(landed):
    slots, width = landed.shape[2], landed.shape[4]
    return pl.pallas_call(
        settle_kernel,
        grid=(slots,),
        out_shape=jax.ShapeDtypeStruct((slots, width, width), F32),
        in_specs=[VMEM],
        out_specs=pl.BlockSpec((1, width, width), lambda s: (s, 0, 0)),
        compiler_params=pltpu.CompilerParams(vmem_limit_bytes=16 * 2**20),
        cost_estimate=pl.CostEstimate(flops=2**30, bytes_accessed=0, transcendentals=0),
        name="settle",
    )(landed)


def join_kernel(*refs):
    pieces, outs = refs[:4], refs[4:]
    rows = pieces[0].shape[0] // len(outs)
    for n, out in enumerate(outs):
        for i in range(4):
            out[i * rows : (i + 1) * rows, :] = pieces[i][n * rows : (n + 1) * rows, :]


def join(pieces, count):
    rows, cols = pieces[0].shape
    return pl.pallas_call(
        join_kernel,
        out_shape=[jax.ShapeDtypeStruct((4 * rows // count, cols), BF)] * count,
        in_specs=[VMEM] * 4,
        out_specs=[VMEM] * count,
        compiler_params=pltpu.CompilerParams(vmem_limit_bytes=8 * 2**20),
        cost_estimate=pl.CostEstimate(
            flops=0, bytes_accessed=0, transcendentals=0
        ),
        name="join",
    )(*pieces)


def direct(x, level):
    return [x, hop(x, level, 1), hop(x, level, -1), hop(x, level, 2)]


def sides(x, level):
    return hop(x, level, 1), hop(x, level, -1)


def body(panel_v, head_v, head_u, diag_inverse, diag_next, ranks, trail_col):
    tile_size = panel_v.shape[2]
    rank = panel_v.shape[3]
    piece = tile_size // 4
    quarter = rank // 4
    col_id = lax.axis_index("col")
    row_id = lax.axis_index("row")
    core = row_id % 2
    my_y = (row_id // 2) % 4
    my_z = row_id // 8
    on_zero = core == 0

    def pick_core(zero, one):
        return jnp.where(on_zero, zero, one)

    inv_mine = pick_core(diag_inverse[0], diag_inverse[1])
    inv_theirs = other_core(pick_core(diag_inverse[1], diag_inverse[0]))
    inv_pair = jnp.concatenate(
        [pick_core(inv_mine, inv_theirs), pick_core(inv_theirs, inv_mine)], axis=1
    )
    column = join(direct(inv_pair, 0), 1)[0]
    panel_other = other_core(panel_v)
    column, panel_late, ranks, trail_col = lax.optimization_barrier((column, panel_v, ranks, trail_col))
    inverse = direct(column, 1)
    own_core = core.astype(jnp.int32)[None]
    cols = jnp.arange(rank)[None, :]
    tiles = trail_col[0]
    slots = tiles.shape[1]
    numbers = jnp.concatenate([ranks[:, 0], tiles.reshape(-1)])
    numbers_other = other_core(numbers.astype(F32)[None])[0].astype(jnp.int32)

    def masked(panels, limits):
        kept = [jnp.where(cols < limits[p], panels[p, 0], jnp.zeros((), BF)) for p in range(2)]
        return pick_core(*kept)

    mine = masked(panel_late, numbers)
    theirs = masked(panel_other, numbers_other)
    rights = [pick_core(mine, theirs), pick_core(theirs, mine), pick_core(head_v, head_u)]
    where = jnp.stack([my_z, my_y, col_id, core]).astype(jnp.int32)
    solved, *thin_parts = solve(where, inverse, rights)

    thin_before = along_x(thin_parts[1], 1)
    thin_after = along_x(thin_parts[3], -1)
    thin_opposite = along_x(thin_parts[2], 2)
    thin_before, thin_after, sent = lax.optimization_barrier((thin_before, thin_after, solved))
    thin = jnp.concatenate([thin_parts[0], thin_before, thin_after, thin_opposite], axis=1)
    line0, line1 = join(direct(thin, 0), 2)
    x_before, x_after, x_opposite = along_x(sent, 1), along_x(sent, -1), along_x(sent, 2)
    line1, x_before, x_after, x_opposite = lax.optimization_barrier(
        (line1, x_before, x_after, x_opposite)
    )
    before0, after0 = lax.optimization_barrier(sides(line0, 1))
    before1, after1 = lax.optimization_barrier(sides(line1, 1))
    gathered0 = [line0, before0, after0, hop(before0, 1, 1)]
    whole, small = couple([solved, x_before, x_after, x_opposite])
    early0 = multiply(whole, gathered0[:3])
    after1, small, early0 = lax.optimization_barrier((after1, small, early0))
    gathered1 = [line1, before1, after1, hop(after1, 1, -1)]
    small_other = other_core(small)
    mats, coupling, gram_h = finish(own_core, small, small_other)

    late, _ = lax.optimization_barrier((solved, gathered0[1]))
    passed = other_core(
        jnp.concatenate(
            [
                pick_core(late[:, rank : 2 * rank], late[:, :rank]),
                late[:, 2 * rank :],
            ],
            axis=1,
        )
    )
    own = pick_core(late[:, :rank], late[:, rank : 2 * rank])
    factor_first = pick_core(own, passed[:, :rank])
    factor_second = pick_core(passed[:, :rank], own)
    head_image = pick_core(passed[:, rank:], late[:, 2 * rank :])

    other_tiles = numbers_other[2:].reshape(tiles.shape)
    j = jnp.stack([pick_core(tiles, other_tiles), pick_core(other_tiles, tiles)]).reshape(2, -1)
    sy = slot_of(((j // 2) % 4 - my_y) % 4)
    sz = slot_of((j // 8 - my_z) % 4)
    places = (pick_core(sz, sy) * 4 + pick_core(sy, sz)) * 2 + j % 2
    early1 = multiply(whole, gathered1[:3])
    picked = pick(places, mats, whole, gathered0[3], gathered1[3], early0, early1)
    upper, _ = lax.optimization_barrier((head_u, picked))
    band = tile_size // 32
    upper_band = lax.dynamic_slice_in_dim(upper, row_id * band, band, 0)
    upper_piece = lax.dynamic_slice_in_dim(upper, col_id * piece, piece, 0)
    next_diagonal = update(gram_h, upper_band, upper_piece, diag_next)
    chip_groups = [[(2 * chip + m) * 4 + c for m in range(2) for c in range(4)] for chip in range(16)]
    landed = lax.all_to_all(
        picked.reshape(8, slots, quarter, 2 * rank),
        ("row", "col"),
        0,
        0,
        axis_index_groups=chip_groups,
        tiled=True,
    )
    cores = settle(landed.reshape(2, 4, slots, quarter, 2 * rank))
    trail_cores = cores.reshape(1, 1, slots, 2 * rank, 2 * rank)
    return (
        factor_first[None],
        factor_second[None],
        coupling[None],
        head_image,
        next_diagonal,
        trail_cores,
    )


def solution(mesh):
    return jax.shard_map(
        body,
        mesh=mesh,
        in_specs=(
            P(None, "row", None, None),
            P(),
            P(),
            P(None, "col", "row"),
            P("row", "col"),
            P(None, "row"),
            P("row", None, None),
        ),
        out_specs=(
            P("row", "col", None),
            P("row", "col", None),
            P("row", None, None),
            P("col", None),
            P("row", "col"),
            P("row", "col", None, None, None),
        ),
        check_vma=False,
    )
```

```python
import jax
import jax.numpy as jnp
from jax import lax
from jax.experimental import pallas as pl
from jax.experimental.pallas import tpu as pltpu
from jax.sharding import PartitionSpec as P

BF = jnp.bfloat16
F32 = jnp.float32


def row_at(z, y, core):
    return ((z % 4) * 4 + (y % 4)) * 2 + core


def other_core(x):
    pairs = [(row_at(z, y, k), row_at(z, y, 1 - k)) for z in range(4) for y in range(4) for k in range(2)]
    return lax.ppermute(x, "row", pairs)


def along_x(x, step):
    pairs = []
    for row in range(32):
        for c in range(4):
            d = step if row % 2 == 0 else -step
            pairs.append((row * 4 + c, row * 4 + (c + d) % 4))
    return lax.ppermute(x, ("row", "col"), pairs)


def hop(x, level, step):
    pairs = []
    for z in range(4):
        for y in range(4):
            for k in range(2):
                dz = step if k != level else 0
                dy = step if k == level else 0
                pairs.append((row_at(z, y, k), row_at(z + dz, y + dy, k)))
    return lax.ppermute(x, "row", pairs)


def slot_of(distance):
    return jnp.where(distance % 2 == 0, distance // 2 * 3, jnp.where(distance == 3, 1, 2))


DISTANCE = (0, 3, 1, 2)
VMEM = pl.BlockSpec(memory_space=pltpu.VMEM)
SMEM = pl.BlockSpec(memory_space=pltpu.SMEM)
ANY = pl.BlockSpec(memory_space=pl.ANY)
HBM = pl.BlockSpec(memory_space=pltpu.HBM)


def unit(size):
    rows = lax.broadcasted_iota(jnp.int32, (size, size), 0)
    cols = lax.broadcasted_iota(jnp.int32, (size, size), 1)
    return jnp.where(rows == cols, 1.0, 0.0).astype(BF)


def flip(x):
    return lax.dot_general(
        unit(x.shape[1]), x, (((1,), (1,)), ((), ())), preferred_element_type=F32
    )


def copy_all(pairs, sems, base=0):
    copies = [pltpu.make_async_copy(src, dst, sems.at[base + i]) for i, (src, dst) in enumerate(pairs)]
    for copy in copies:
        copy.start()
    return copies


def solve_kernel(where, *refs):
    pieces, (right0, right1, right2), (out, *thin), (whole, turned) = (
        refs[:4],
        refs[4:7],
        refs[7:12],
        refs[12:],
    )
    piece = out.shape[0]
    width = whole.shape[1] // 16
    on_zero = where[3] == 0
    for slow in range(4):
        for fast in range(4):
            dz = jnp.where(on_zero, DISTANCE[slow], DISTANCE[fast])
            dy = jnp.where(on_zero, DISTANCE[fast], DISTANCE[slow])
            chip = lax.rem(where[0] + dz, 4) * 4 + lax.rem(where[1] + dy, 4)
            start = pl.multiple_of(chip * width, width)
            whole[:, pl.ds(start, width)] = pieces[slow][fast * piece : (fast + 1) * piece, :]
    rank = right0.shape[1]
    for n, right in enumerate((right0, right1, right2)):
        out[:, n * rank : (n + 1) * rank] = jnp.dot(
            whole[...], right[...], preferred_element_type=F32
        ).astype(BF)
    turned[...] = flip(out[:, : 2 * rank]).astype(BF)
    quarter = rank // 4
    half = quarter // 2
    for step in range(4):
        q = lax.rem(where[2] + jnp.where(on_zero, step, 4 - step), 4)
        for h in range(2):
            for a in range(2):
                start = pl.multiple_of(a * rank + q * quarter + h * half, half)
                at = (2 * h + a) * half
                thin[step][at : at + half, :] = turned[pl.ds(start, half), :]


def solve(where, pieces, rights):
    piece = pieces[0].shape[0] // 4
    tile_size, rank = rights[0].shape
    return pl.pallas_call(
        solve_kernel,
        out_shape=[jax.ShapeDtypeStruct((piece, 3 * rank), BF)]
        + [jax.ShapeDtypeStruct((rank // 2, piece), BF)] * 4,
        in_specs=[SMEM] + [VMEM] * 7,
        out_specs=[VMEM] * 5,
        scratch_shapes=[
            pltpu.VMEM((piece, tile_size), BF),
            pltpu.VMEM((2 * rank, piece), BF),
        ],
        compiler_params=pltpu.CompilerParams(vmem_limit_bytes=16 * 2**20),
        cost_estimate=pl.CostEstimate(
            flops=2 * piece * tile_size * 3 * rank, bytes_accessed=0, transcendentals=0
        ),
        name="solve",
    )(where, *pieces, *rights)


def multiply_kernel(*refs):
    count = len(refs) - 4
    whole, pieces, (out, held, sems) = refs[0], refs[1 : 1 + count], refs[1 + count :]
    rows = pieces[0].shape[0]
    copies = copy_all(
        [(p, held.at[pl.ds(i * rows, rows)]) for i, p in enumerate(pieces)], sems
    )
    for copy in copies:
        copy.wait()
    out[...] = jnp.dot(held[...], whole[...], preferred_element_type=F32)


def multiply(whole, pieces):
    depth, width = whole.shape
    rows = pieces[0].shape[0]
    count = len(pieces)
    return pl.pallas_call(
        multiply_kernel,
        out_shape=jax.ShapeDtypeStruct((count * rows, width), F32),
        in_specs=[VMEM] + [ANY] * count,
        out_specs=VMEM,
        scratch_shapes=[
            pltpu.VMEM((count * rows, depth), BF),
            pltpu.SemaphoreType.DMA((count,)),
        ],
        compiler_params=pltpu.CompilerParams(vmem_limit_bytes=16 * 2**20),
        cost_estimate=pl.CostEstimate(
            flops=2 * count * rows * depth * width, bytes_accessed=0, transcendentals=0
        ),
        name="multiply",
    )(whole, *pieces)


def pick_kernel(
    places, mats, whole, piece0, piece1, early0, early1, out, late0, late1, heads, staged, sems
):
    rows = piece0.shape[0]
    done = late0.shape[0] - rows
    copies = copy_all(
        [
            (early0.at[pl.ds(0, done)], late0.at[pl.ds(0, done)]),
            (early0.at[pl.ds(done, rows)], late1.at[pl.ds(0, rows)]),
            (early1, late1.at[pl.ds(rows, done - rows)]),
        ],
        sems,
        2,
    )
    late0[done:, :] = jnp.dot(piece0[...], whole[...], preferred_element_type=F32)
    late1[done:, :] = jnp.dot(piece1[...], whole[...], preferred_element_type=F32)
    for copy in copies:
        copy.wait()
    products = (late0, late1)
    rank = mats.shape[1]
    half = rank // 8
    count = places.shape[1]
    leaving = []
    for a in range(2):
        at = [pl.ds(pl.multiple_of(places[a, i] * half, half), half) for i in range(count)]
        for i in range(count):
            for h in range(2):
                rows = slice((2 * i + h) * half, (2 * i + h + 1) * half)
                heads[rows, :] = products[h][at[i], 2 * rank :].astype(BF)
        low = jnp.dot(heads[...], mats[a], preferred_element_type=F32)
        for i in range(count):
            for h in range(2):
                mine = low[(2 * i + h) * half : (2 * i + h + 1) * half, :]
                direct = products[h][at[i], a * rank : (a + 1) * rank]
                rows = slice(h * half, (h + 1) * half)
                staged[a, i, rows, :rank] = (mine[:, :rank] + direct).astype(BF)
                staged[a, i, rows, rank:] = mine[:, rank:].astype(BF)
        leaving += copy_all([(staged.at[a], out.at[a])], sems, a)
    for copy in leaving:
        copy.wait()


def pick(places, mats, whole, piece0, piece1, early0, early1):
    count = places.shape[1]
    rank = mats.shape[1]
    shape = (2, count, rank // 4, 2 * rank)
    full = (4 * piece0.shape[0], early0.shape[1])
    return pl.pallas_call(
        pick_kernel,
        out_shape=jax.ShapeDtypeStruct(shape, BF),
        in_specs=[SMEM] + [VMEM] * 6,
        out_specs=HBM,
        scratch_shapes=[
            pltpu.VMEM(full, F32),
            pltpu.VMEM(full, F32),
            pltpu.VMEM((count * rank // 4, rank), BF),
            pltpu.VMEM(shape, BF),
            pltpu.SemaphoreType.DMA((5,)),
        ],
        compiler_params=pltpu.CompilerParams(vmem_limit_bytes=28 * 2**20),
        cost_estimate=pl.CostEstimate(
            flops=2**30, bytes_accessed=0, transcendentals=0
        ),
        name="pick",
    )(places, mats, whole, piece0, piece1, early0, early1)


def couple_kernel(*refs):
    parts, whole, out = refs[:4], refs[4], refs[5]
    rank = out.shape[1]
    size = parts[0].shape[0]
    for i, part in enumerate(parts):
        whole[i * size : (i + 1) * size, :] = part[...]
        term = lax.dot_general(
            part[...], part[:, 2 * rank :], (((0,), (0,)), ((), ())), preferred_element_type=F32
        )
        out[...] = term if i == 0 else out[...] + term


def couple(parts):
    size, width = parts[0].shape
    return pl.pallas_call(
        couple_kernel,
        out_shape=[
            jax.ShapeDtypeStruct((4 * size, width), BF),
            jax.ShapeDtypeStruct((width, width // 3), F32),
        ],
        in_specs=[VMEM] * 4,
        out_specs=[VMEM] * 2,
        compiler_params=pltpu.CompilerParams(vmem_limit_bytes=16 * 2**20),
        cost_estimate=pl.CostEstimate(
            flops=2 * 4 * size * width * width // 3, bytes_accessed=0, transcendentals=0
        ),
        name="couple",
    )(*parts)


def split(x):
    high = x.astype(BF)
    return high, (x - high.astype(F32)).astype(BF)


def by_rows(a, b):
    return lax.dot_general(a, b, (((1,), (1,)), ((), ())), preferred_element_type=F32)


def finish_kernel(core, small, other, mats, coupling, gram):
    rank = small.shape[1]
    last = slice(2 * rank, 3 * rank)
    on_zero = core[0] == 0
    for a in range(2):
        rows = slice(a * rank, (a + 1) * rank)
        high, low = split(small[rows, :])
        gram_high, gram_low = split(other[last, :])
        weight = by_rows(gram_high, high) + by_rows(gram_high, low) + by_rows(gram_low, high)
        mats[a, :, :rank] = jnp.where(on_zero, weight, 0.0).astype(BF)
        mats[a, :, rank:] = (-flip(other[rows, :].astype(BF))).astype(BF)
    coupling[...] = jnp.where(on_zero, small[:rank, :], other[rank : 2 * rank, :])
    gram[...] = jnp.where(on_zero, small[last, :], other[last, :])


def finish(core, small, other):
    rank = small.shape[1]
    return pl.pallas_call(
        finish_kernel,
        out_shape=[
            jax.ShapeDtypeStruct((2, rank, 2 * rank), BF),
            jax.ShapeDtypeStruct((rank, rank), F32),
            jax.ShapeDtypeStruct((rank, rank), F32),
        ],
        in_specs=[SMEM] + [VMEM] * 2,
        out_specs=[VMEM] * 3,
        compiler_params=pltpu.CompilerParams(vmem_limit_bytes=8 * 2**20),
        cost_estimate=pl.CostEstimate(flops=2**28, bytes_accessed=0, transcendentals=0),
        name="finish",
    )(core, small, other)


def update_kernel(gram, band, piece, before, after):
    gram_high, gram_low = split(gram[...])
    middle = jnp.dot(band[...], gram_high, preferred_element_type=F32) + jnp.dot(
        band[...], gram_low, preferred_element_type=F32
    )
    high, low = split(middle)
    after[...] = before[...] - (by_rows(high, piece[...]) + by_rows(low, piece[...]))


def update(gram, band, piece, before):
    return pl.pallas_call(
        update_kernel,
        out_shape=jax.ShapeDtypeStruct(before.shape, F32),
        in_specs=[VMEM] * 4,
        out_specs=VMEM,
        compiler_params=pltpu.CompilerParams(vmem_limit_bytes=8 * 2**20),
        cost_estimate=pl.CostEstimate(flops=2**26, bytes_accessed=0, transcendentals=0),
        name="update",
    )(gram, band, piece, before)


def settle_kernel(landed, out):
    rank = landed.shape[4] // 2
    for p in range(2):
        x = landed[p, :, pl.program_id(0)].reshape(rank, 2 * rank)
        direct = flip(x[:, :rank])
        crossed = flip(x[:, rank:])
        cols = slice(p * rank, (p + 1) * rank)
        out[0, :rank, cols] = direct if p == 0 else crossed
        out[0, rank:, cols] = crossed if p == 0 else direct


def settle(landed):
    slots, width = landed.shape[2], landed.shape[4]
    return pl.pallas_call(
        settle_kernel,
        grid=(slots,),
        out_shape=jax.ShapeDtypeStruct((slots, width, width), F32),
        in_specs=[VMEM],
        out_specs=pl.BlockSpec((1, width, width), lambda s: (s, 0, 0)),
        compiler_params=pltpu.CompilerParams(vmem_limit_bytes=16 * 2**20),
        cost_estimate=pl.CostEstimate(flops=2**30, bytes_accessed=0, transcendentals=0),
        name="settle",
    )(landed)


def join_kernel(*refs):
    pieces, outs = refs[:4], refs[4:]
    rows = pieces[0].shape[0] // len(outs)
    for n, out in enumerate(outs):
        for i in range(4):
            out[i * rows : (i + 1) * rows, :] = pieces[i][n * rows : (n + 1) * rows, :]


def join(pieces, count):
    rows, cols = pieces[0].shape
    return pl.pallas_call(
        join_kernel,
        out_shape=[jax.ShapeDtypeStruct((4 * rows // count, cols), BF)] * count,
        in_specs=[VMEM] * 4,
        out_specs=[VMEM] * count,
        compiler_params=pltpu.CompilerParams(vmem_limit_bytes=8 * 2**20),
        cost_estimate=pl.CostEstimate(
            flops=0, bytes_accessed=0, transcendentals=0
        ),
        name="join",
    )(*pieces)


def direct(x, level):
    return [x, hop(x, level, 1), hop(x, level, -1), hop(x, level, 2)]


def sides(x, level):
    return hop(x, level, 1), hop(x, level, -1)


def body(panel_v, head_v, head_u, diag_inverse, diag_next, ranks, trail_col):
    tile_size = panel_v.shape[2]
    rank = panel_v.shape[3]
    piece = tile_size // 4
    quarter = rank // 4
    col_id = lax.axis_index("col")
    row_id = lax.axis_index("row")
    core = row_id % 2
    my_y = (row_id // 2) % 4
    my_z = row_id // 8
    on_zero = core == 0

    def pick_core(zero, one):
        return jnp.where(on_zero, zero, one)

    inv_mine = pick_core(diag_inverse[0], diag_inverse[1])
    inv_theirs = other_core(pick_core(diag_inverse[1], diag_inverse[0]))
    inv_pair = jnp.concatenate(
        [pick_core(inv_mine, inv_theirs), pick_core(inv_theirs, inv_mine)], axis=1
    )
    column = join(direct(inv_pair, 0), 1)[0]
    panel_other = other_core(panel_v)
    column, panel_late, ranks, trail_col = lax.optimization_barrier((column, panel_v, ranks, trail_col))
    inverse = direct(column, 1)
    own_core = core.astype(jnp.int32)[None]
    cols = jnp.arange(rank)[None, :]
    tiles = trail_col[0]
    slots = tiles.shape[1]
    numbers = jnp.concatenate([ranks[:, 0], tiles.reshape(-1)])
    numbers_other = other_core(numbers.astype(F32)[None])[0].astype(jnp.int32)

    def masked(panels, limits):
        kept = [jnp.where(cols < limits[p], panels[p, 0], jnp.zeros((), BF)) for p in range(2)]
        return pick_core(*kept)

    mine = masked(panel_late, numbers)
    theirs = masked(panel_other, numbers_other)
    rights = [pick_core(mine, theirs), pick_core(theirs, mine), pick_core(head_v, head_u)]
    where = jnp.stack([my_z, my_y, col_id, core]).astype(jnp.int32)
    solved, *thin_parts = solve(where, inverse, rights)

    thin_before = along_x(thin_parts[1], 1)
    thin_after = along_x(thin_parts[3], -1)
    thin_opposite = along_x(thin_parts[2], 2)
    thin_before, thin_after, sent = lax.optimization_barrier((thin_before, thin_after, solved))
    thin = jnp.concatenate([thin_parts[0], thin_before, thin_after, thin_opposite], axis=1)
    line0, line1 = join(direct(thin, 0), 2)
    x_before, x_after, x_opposite = along_x(sent, 1), along_x(sent, -1), along_x(sent, 2)
    line1, x_before, x_after, x_opposite = lax.optimization_barrier(
        (line1, x_before, x_after, x_opposite)
    )
    before0, after0 = lax.optimization_barrier(sides(line0, 1))
    before1, after1 = lax.optimization_barrier(sides(line1, 1))
    gathered0 = [line0, before0, after0, hop(before0, 1, 1)]
    whole, small = couple([solved, x_before, x_after, x_opposite])
    early0 = multiply(whole, gathered0[:3] + [line1])
    after1, small, early0 = lax.optimization_barrier((after1, small, early0))
    gathered1 = [line1, before1, after1, hop(after1, 1, -1)]
    small_other = other_core(small)
    mats, coupling, gram_h = finish(own_core, small, small_other)

    late, _ = lax.optimization_barrier((solved, gathered0[1]))
    passed = other_core(
        jnp.concatenate(
            [
                pick_core(late[:, rank : 2 * rank], late[:, :rank]),
                late[:, 2 * rank :],
            ],
            axis=1,
        )
    )
    own = pick_core(late[:, :rank], late[:, rank : 2 * rank])
    factor_first = pick_core(own, passed[:, :rank])
    factor_second = pick_core(passed[:, :rank], own)
    head_image = pick_core(passed[:, rank:], late[:, 2 * rank :])

    other_tiles = numbers_other[2:].reshape(tiles.shape)
    j = jnp.stack([pick_core(tiles, other_tiles), pick_core(other_tiles, tiles)]).reshape(2, -1)
    sy = slot_of(((j // 2) % 4 - my_y) % 4)
    sz = slot_of((j // 8 - my_z) % 4)
    places = (pick_core(sz, sy) * 4 + pick_core(sy, sz)) * 2 + j % 2
    early1 = multiply(whole, gathered1[1:3])
    picked = pick(places, mats, whole, gathered0[3], gathered1[3], early0, early1)
    upper, _ = lax.optimization_barrier((head_u, picked))
    band = tile_size // 32
    upper_band = lax.dynamic_slice_in_dim(upper, row_id * band, band, 0)
    upper_piece = lax.dynamic_slice_in_dim(upper, col_id * piece, piece, 0)
    next_diagonal = update(gram_h, upper_band, upper_piece, diag_next)
    chip_groups = [[(2 * chip + m) * 4 + c for m in range(2) for c in range(4)] for chip in range(16)]
    landed = lax.all_to_all(
        picked.reshape(8, slots, quarter, 2 * rank),
        ("row", "col"),
        0,
        0,
        axis_index_groups=chip_groups,
        tiled=True,
    )
    cores = settle(landed.reshape(2, 4, slots, quarter, 2 * rank))
    trail_cores = cores.reshape(1, 1, slots, 2 * rank, 2 * rank)
    return (
        factor_first[None],
        factor_second[None],
        coupling[None],
        head_image,
        next_diagonal,
        trail_cores,
    )


def solution(mesh):
    return jax.shard_map(
        body,
        mesh=mesh,
        in_specs=(
            P(None, "row", None, None),
            P(),
            P(),
            P(None, "col", "row"),
            P("row", "col"),
            P(None, "row"),
            P("row", None, None),
        ),
        out_specs=(
            P("row", "col", None),
            P("row", "col", None),
            P("row", None, None),
            P("col", None),
            P("row", "col"),
            P("row", "col", None, None, None),
        ),
        check_vma=False,
    )
```

```python
import jax
import jax.numpy as jnp
from jax import lax
from jax.experimental import pallas as pl
from jax.experimental.pallas import tpu as pltpu
from jax.sharding import PartitionSpec as P

BF = jnp.bfloat16
F32 = jnp.float32


def row_at(z, y, core):
    return ((z % 4) * 4 + (y % 4)) * 2 + core


def other_core(x):
    pairs = [(row_at(z, y, k), row_at(z, y, 1 - k)) for z in range(4) for y in range(4) for k in range(2)]
    return lax.ppermute(x, "row", pairs)


def along_x(x, step):
    pairs = []
    for row in range(32):
        for c in range(4):
            d = step if row % 2 == 0 else -step
            pairs.append((row * 4 + c, row * 4 + (c + d) % 4))
    return lax.ppermute(x, ("row", "col"), pairs)


def hop(x, level, step):
    pairs = []
    for z in range(4):
        for y in range(4):
            for k in range(2):
                dz = step if k != level else 0
                dy = step if k == level else 0
                pairs.append((row_at(z, y, k), row_at(z + dz, y + dy, k)))
    return lax.ppermute(x, "row", pairs)


def slot_of(distance):
    return jnp.where(distance % 2 == 0, distance // 2 * 3, jnp.where(distance == 3, 1, 2))


DISTANCE = (0, 3, 1, 2)
VMEM = pl.BlockSpec(memory_space=pltpu.VMEM)
SMEM = pl.BlockSpec(memory_space=pltpu.SMEM)
ANY = pl.BlockSpec(memory_space=pl.ANY)
HBM = pl.BlockSpec(memory_space=pltpu.HBM)


def unit(size):
    rows = lax.broadcasted_iota(jnp.int32, (size, size), 0)
    cols = lax.broadcasted_iota(jnp.int32, (size, size), 1)
    return jnp.where(rows == cols, 1.0, 0.0).astype(BF)


def flip(x):
    return lax.dot_general(
        unit(x.shape[1]), x, (((1,), (1,)), ((), ())), preferred_element_type=F32
    )


def copy_all(pairs, sems, base=0):
    copies = [pltpu.make_async_copy(src, dst, sems.at[base + i]) for i, (src, dst) in enumerate(pairs)]
    for copy in copies:
        copy.start()
    return copies


def solve_kernel(where, *refs):
    pieces, (right0, right1, right2), (out, *thin), (whole, turned) = (
        refs[:4],
        refs[4:7],
        refs[7:12],
        refs[12:],
    )
    piece = out.shape[0]
    width = whole.shape[1] // 16
    on_zero = where[3] == 0
    for slow in range(4):
        for fast in range(4):
            dz = jnp.where(on_zero, DISTANCE[slow], DISTANCE[fast])
            dy = jnp.where(on_zero, DISTANCE[fast], DISTANCE[slow])
            chip = lax.rem(where[0] + dz, 4) * 4 + lax.rem(where[1] + dy, 4)
            start = pl.multiple_of(chip * width, width)
            whole[:, pl.ds(start, width)] = pieces[slow][fast * piece : (fast + 1) * piece, :]
    rank = right0.shape[1]
    for n, right in enumerate((right0, right1, right2)):
        out[:, n * rank : (n + 1) * rank] = jnp.dot(
            whole[...], right[...], preferred_element_type=F32
        ).astype(BF)
    turned[...] = flip(out[:, : 2 * rank]).astype(BF)
    quarter = rank // 4
    half = quarter // 2
    for step in range(4):
        q = lax.rem(where[2] + jnp.where(on_zero, step, 4 - step), 4)
        for h in range(2):
            for a in range(2):
                start = pl.multiple_of(a * rank + q * quarter + h * half, half)
                at = (2 * h + a) * half
                thin[step][at : at + half, :] = turned[pl.ds(start, half), :]


def solve(where, pieces, rights):
    piece = pieces[0].shape[0] // 4
    tile_size, rank = rights[0].shape
    return pl.pallas_call(
        solve_kernel,
        out_shape=[jax.ShapeDtypeStruct((piece, 3 * rank), BF)]
        + [jax.ShapeDtypeStruct((rank // 2, piece), BF)] * 4,
        in_specs=[SMEM] + [VMEM] * 7,
        out_specs=[VMEM] * 5,
        scratch_shapes=[
            pltpu.VMEM((piece, tile_size), BF),
            pltpu.VMEM((2 * rank, piece), BF),
        ],
        compiler_params=pltpu.CompilerParams(vmem_limit_bytes=16 * 2**20),
        cost_estimate=pl.CostEstimate(
            flops=2 * piece * tile_size * 3 * rank, bytes_accessed=0, transcendentals=0
        ),
        name="solve",
    )(where, *pieces, *rights)


def multiply_kernel(*refs):
    count = len(refs) - 4
    whole, pieces, (out, held, sems) = refs[0], refs[1 : 1 + count], refs[1 + count :]
    rows = pieces[0].shape[0]
    copies = copy_all(
        [(p, held.at[pl.ds(i * rows, rows)]) for i, p in enumerate(pieces)], sems
    )
    for copy in copies:
        copy.wait()
    out[...] = jnp.dot(held[...], whole[...], preferred_element_type=F32)


def multiply(whole, pieces):
    depth, width = whole.shape
    rows = pieces[0].shape[0]
    count = len(pieces)
    return pl.pallas_call(
        multiply_kernel,
        out_shape=jax.ShapeDtypeStruct((count * rows, width), F32),
        in_specs=[VMEM] + [ANY] * count,
        out_specs=VMEM,
        scratch_shapes=[
            pltpu.VMEM((count * rows, depth), BF),
            pltpu.SemaphoreType.DMA((count,)),
        ],
        compiler_params=pltpu.CompilerParams(vmem_limit_bytes=16 * 2**20),
        cost_estimate=pl.CostEstimate(
            flops=2 * count * rows * depth * width, bytes_accessed=0, transcendentals=0
        ),
        name="multiply",
    )(whole, *pieces)


def pick_kernel(
    places, mats, whole, piece0, piece1, early0, early1, out, late0, late1, heads, staged, sems
):
    done = early0.shape[0]
    copies = copy_all(
        [(early0, late0.at[pl.ds(0, done)]), (early1, late1.at[pl.ds(0, done)])], sems, 2
    )
    late0[done:, :] = jnp.dot(piece0[...], whole[...], preferred_element_type=F32)
    late1[done:, :] = jnp.dot(piece1[...], whole[...], preferred_element_type=F32)
    for copy in copies:
        copy.wait()
    products = (late0, late1)
    rank = mats.shape[1]
    half = rank // 8
    count = places.shape[1]
    leaving = []
    for a in range(2):
        at = [pl.ds(pl.multiple_of(places[a, i] * half, half), half) for i in range(count)]
        for i in range(count):
            for h in range(2):
                rows = slice((2 * i + h) * half, (2 * i + h + 1) * half)
                heads[rows, :] = products[h][at[i], 2 * rank :].astype(BF)
        low = jnp.dot(heads[...], mats[a], preferred_element_type=F32)
        for i in range(count):
            for h in range(2):
                mine = low[(2 * i + h) * half : (2 * i + h + 1) * half, :]
                direct = products[h][at[i], a * rank : (a + 1) * rank]
                rows = slice(h * half, (h + 1) * half)
                staged[a, i, rows, :rank] = (mine[:, :rank] + direct).astype(BF)
                staged[a, i, rows, rank:] = mine[:, rank:].astype(BF)
        leaving += copy_all([(staged.at[a], out.at[a])], sems, a)
    for copy in leaving:
        copy.wait()


def pick(places, mats, whole, piece0, piece1, early0, early1):
    count = places.shape[1]
    rank = mats.shape[1]
    shape = (2, count, rank // 4, 2 * rank)
    full = (early0.shape[0] + piece0.shape[0], early0.shape[1])
    return pl.pallas_call(
        pick_kernel,
        out_shape=jax.ShapeDtypeStruct(shape, BF),
        in_specs=[SMEM] + [VMEM] * 6,
        out_specs=HBM,
        scratch_shapes=[
            pltpu.VMEM(full, F32),
            pltpu.VMEM(full, F32),
            pltpu.VMEM((count * rank // 4, rank), BF),
            pltpu.VMEM(shape, BF),
            pltpu.SemaphoreType.DMA((4,)),
        ],
        compiler_params=pltpu.CompilerParams(vmem_limit_bytes=28 * 2**20),
        cost_estimate=pl.CostEstimate(
            flops=2**30, bytes_accessed=0, transcendentals=0
        ),
        name="pick",
    )(places, mats, whole, piece0, piece1, early0, early1)


def couple_kernel(*refs):
    parts, whole, out = refs[:4], refs[4], refs[5]
    rank = out.shape[1]
    size = parts[0].shape[0]
    for i, part in enumerate(parts):
        whole[i * size : (i + 1) * size, :] = part[...]
        term = lax.dot_general(
            part[...], part[:, 2 * rank :], (((0,), (0,)), ((), ())), preferred_element_type=F32
        )
        out[...] = term if i == 0 else out[...] + term


def couple(parts):
    size, width = parts[0].shape
    return pl.pallas_call(
        couple_kernel,
        out_shape=[
            jax.ShapeDtypeStruct((4 * size, width), BF),
            jax.ShapeDtypeStruct((width, width // 3), F32),
        ],
        in_specs=[VMEM] * 4,
        out_specs=[VMEM] * 2,
        compiler_params=pltpu.CompilerParams(vmem_limit_bytes=16 * 2**20),
        cost_estimate=pl.CostEstimate(
            flops=2 * 4 * size * width * width // 3, bytes_accessed=0, transcendentals=0
        ),
        name="couple",
    )(*parts)


def split(x):
    high = x.astype(BF)
    return high, (x - high.astype(F32)).astype(BF)


def by_rows(a, b):
    return lax.dot_general(a, b, (((1,), (1,)), ((), ())), preferred_element_type=F32)


def finish_kernel(core, small, other, mats, coupling, gram):
    rank = small.shape[1]
    last = slice(2 * rank, 3 * rank)
    on_zero = core[0] == 0
    for a in range(2):
        rows = slice(a * rank, (a + 1) * rank)
        high, low = split(small[rows, :])
        gram_high, gram_low = split(other[last, :])
        weight = by_rows(gram_high, high) + by_rows(gram_high, low) + by_rows(gram_low, high)
        mats[a, :, :rank] = jnp.where(on_zero, weight, 0.0).astype(BF)
        mats[a, :, rank:] = (-flip(other[rows, :].astype(BF))).astype(BF)
    coupling[...] = jnp.where(on_zero, small[:rank, :], other[rank : 2 * rank, :])
    gram[...] = jnp.where(on_zero, small[last, :], other[last, :])


def finish(core, small, other):
    rank = small.shape[1]
    return pl.pallas_call(
        finish_kernel,
        out_shape=[
            jax.ShapeDtypeStruct((2, rank, 2 * rank), BF),
            jax.ShapeDtypeStruct((rank, rank), F32),
            jax.ShapeDtypeStruct((rank, rank), F32),
        ],
        in_specs=[SMEM] + [VMEM] * 2,
        out_specs=[VMEM] * 3,
        compiler_params=pltpu.CompilerParams(vmem_limit_bytes=8 * 2**20),
        cost_estimate=pl.CostEstimate(flops=2**28, bytes_accessed=0, transcendentals=0),
        name="finish",
    )(core, small, other)


def update_kernel(gram, band, piece, before, after):
    gram_high, gram_low = split(gram[...])
    middle = jnp.dot(band[...], gram_high, preferred_element_type=F32) + jnp.dot(
        band[...], gram_low, preferred_element_type=F32
    )
    high, low = split(middle)
    after[...] = before[...] - (by_rows(high, piece[...]) + by_rows(low, piece[...]))


def update(gram, band, piece, before):
    return pl.pallas_call(
        update_kernel,
        out_shape=jax.ShapeDtypeStruct(before.shape, F32),
        in_specs=[VMEM] * 4,
        out_specs=VMEM,
        compiler_params=pltpu.CompilerParams(vmem_limit_bytes=8 * 2**20),
        cost_estimate=pl.CostEstimate(flops=2**26, bytes_accessed=0, transcendentals=0),
        name="update",
    )(gram, band, piece, before)


def settle_kernel(landed, out):
    rank = landed.shape[4] // 2
    for p in range(2):
        x = landed[p, :, pl.program_id(0)].reshape(rank, 2 * rank)
        direct = flip(x[:, :rank])
        crossed = flip(x[:, rank:])
        cols = slice(p * rank, (p + 1) * rank)
        out[0, :rank, cols] = direct if p == 0 else crossed
        out[0, rank:, cols] = crossed if p == 0 else direct


def settle(landed):
    slots, width = landed.shape[2], landed.shape[4]
    return pl.pallas_call(
        settle_kernel,
        grid=(slots,),
        out_shape=jax.ShapeDtypeStruct((slots, width, width), F32),
        in_specs=[VMEM],
        out_specs=pl.BlockSpec((1, width, width), lambda s: (s, 0, 0)),
        compiler_params=pltpu.CompilerParams(vmem_limit_bytes=16 * 2**20),
        cost_estimate=pl.CostEstimate(flops=2**30, bytes_accessed=0, transcendentals=0),
        name="settle",
    )(landed)


def join_kernel(*refs):
    pieces, outs = refs[:4], refs[4:]
    rows = pieces[0].shape[0] // len(outs)
    for n, out in enumerate(outs):
        for i in range(4):
            out[i * rows : (i + 1) * rows, :] = pieces[i][n * rows : (n + 1) * rows, :]


def join(pieces, count):
    rows, cols = pieces[0].shape
    return pl.pallas_call(
        join_kernel,
        out_shape=[jax.ShapeDtypeStruct((4 * rows // count, cols), BF)] * count,
        in_specs=[VMEM] * 4,
        out_specs=[VMEM] * count,
        compiler_params=pltpu.CompilerParams(vmem_limit_bytes=8 * 2**20),
        cost_estimate=pl.CostEstimate(
            flops=0, bytes_accessed=0, transcendentals=0
        ),
        name="join",
    )(*pieces)


def direct(x, level):
    return [x, hop(x, level, 1), hop(x, level, -1), hop(x, level, 2)]


def sides(x, level):
    return hop(x, level, 1), hop(x, level, -1)


def body(panel_v, head_v, head_u, diag_inverse, diag_next, ranks, trail_col):
    tile_size = panel_v.shape[2]
    rank = panel_v.shape[3]
    piece = tile_size // 4
    quarter = rank // 4
    col_id = lax.axis_index("col")
    row_id = lax.axis_index("row")
    core = row_id % 2
    my_y = (row_id // 2) % 4
    my_z = row_id // 8
    on_zero = core == 0

    def pick_core(zero, one):
        return jnp.where(on_zero, zero, one)

    inv_mine = pick_core(diag_inverse[0], diag_inverse[1])
    inv_theirs = other_core(pick_core(diag_inverse[1], diag_inverse[0]))
    inv_pair = jnp.concatenate(
        [pick_core(inv_mine, inv_theirs), pick_core(inv_theirs, inv_mine)], axis=1
    )
    column = join(direct(inv_pair, 0), 1)[0]
    panel_other = other_core(panel_v)
    column, panel_late, ranks, trail_col = lax.optimization_barrier((column, panel_v, ranks, trail_col))
    inverse = direct(column, 1)
    own_core = core.astype(jnp.int32)[None]
    cols = jnp.arange(rank)[None, :]
    tiles = trail_col[0]
    slots = tiles.shape[1]
    numbers = jnp.concatenate([ranks[:, 0], tiles.reshape(-1)])
    numbers_other = other_core(numbers.astype(F32)[None])[0].astype(jnp.int32)

    def masked(panels, limits):
        kept = [jnp.where(cols < limits[p], panels[p, 0], jnp.zeros((), BF)) for p in range(2)]
        return pick_core(*kept)

    mine = masked(panel_late, numbers)
    theirs = masked(panel_other, numbers_other)
    rights = [pick_core(mine, theirs), pick_core(theirs, mine), pick_core(head_v, head_u)]
    where = jnp.stack([my_z, my_y, col_id, core]).astype(jnp.int32)
    solved, *thin_parts = solve(where, inverse, rights)

    thin_before = along_x(thin_parts[1], 1)
    thin_after = along_x(thin_parts[3], -1)
    thin_opposite = along_x(thin_parts[2], 2)
    thin_before, thin_after, sent = lax.optimization_barrier((thin_before, thin_after, solved))
    thin = jnp.concatenate([thin_parts[0], thin_before, thin_after, thin_opposite], axis=1)
    line0, line1 = join(direct(thin, 0), 2)
    x_before, x_after, x_opposite = along_x(sent, 1), along_x(sent, -1), along_x(sent, 2)
    line1, x_before, x_after, x_opposite = lax.optimization_barrier(
        (line1, x_before, x_after, x_opposite)
    )
    before0, after0 = lax.optimization_barrier(sides(line0, 1))
    before1, after1 = lax.optimization_barrier(sides(line1, 1))
    gathered0 = [line0, before0, after0, hop(before0, 1, 1)]
    whole, small = couple([solved, x_before, x_after, x_opposite])
    early0 = multiply(whole, gathered0[:3])
    after1, _, _ = lax.optimization_barrier((after1, small, early0))
    gathered1 = [line1, before1, after1, hop(after1, 1, -1)]
    small_other = other_core(small)
    mats, coupling, gram_h = finish(own_core, small, small_other)

    late, _ = lax.optimization_barrier((solved, gathered0[1]))
    passed = other_core(
        jnp.concatenate(
            [
                pick_core(late[:, rank : 2 * rank], late[:, :rank]),
                late[:, 2 * rank :],
            ],
            axis=1,
        )
    )
    own = pick_core(late[:, :rank], late[:, rank : 2 * rank])
    factor_first = pick_core(own, passed[:, :rank])
    factor_second = pick_core(passed[:, :rank], own)
    head_image = pick_core(passed[:, rank:], late[:, 2 * rank :])

    other_tiles = numbers_other[2:].reshape(tiles.shape)
    j = jnp.stack([pick_core(tiles, other_tiles), pick_core(other_tiles, tiles)]).reshape(2, -1)
    sy = slot_of(((j // 2) % 4 - my_y) % 4)
    sz = slot_of((j // 8 - my_z) % 4)
    places = (pick_core(sz, sy) * 4 + pick_core(sy, sz)) * 2 + j % 2
    early1 = multiply(whole, gathered1[:3])
    picked = pick(places, mats, whole, gathered0[3], gathered1[3], early0, early1)
    upper, _ = lax.optimization_barrier((head_u, picked))
    band = tile_size // 32
    upper_band = lax.dynamic_slice_in_dim(upper, row_id * band, band, 0)
    upper_piece = lax.dynamic_slice_in_dim(upper, col_id * piece, piece, 0)
    next_diagonal = update(gram_h, upper_band, upper_piece, diag_next)
    chip_groups = [[(2 * chip + m) * 4 + c for m in range(2) for c in range(4)] for chip in range(16)]
    landed = lax.all_to_all(
        picked.reshape(8, slots, quarter, 2 * rank),
        ("row", "col"),
        0,
        0,
        axis_index_groups=chip_groups,
        tiled=True,
    )
    cores = settle(landed.reshape(2, 4, slots, quarter, 2 * rank))
    trail_cores = cores.reshape(1, 1, slots, 2 * rank, 2 * rank)
    return (
        factor_first[None],
        factor_second[None],
        coupling[None],
        head_image,
        next_diagonal,
        trail_cores,
    )


def solution(mesh):
    return jax.shard_map(
        body,
        mesh=mesh,
        in_specs=(
            P(None, "row", None, None),
            P(),
            P(),
            P(None, "col", "row"),
            P("row", "col"),
            P(None, "row"),
            P("row", None, None),
        ),
        out_specs=(
            P("row", "col", None),
            P("row", "col", None),
            P("row", None, None),
            P("col", None),
            P("row", "col"),
            P("row", "col", None, None, None),
        ),
        check_vma=False,
    )
```
